128 devices in a mesh: mesh: 32 (over x, y, core), band: 4 (over z).
Axes of the slice: x: 4, y: 4, z: 4, core: 2. Of those that a mesh axis runs over, the one named last changes fastest.
Arguments:
- mesh_latent: bfloat16 [65536, 512], P(('mesh', 'band')), may hold values from -6 to 6
- grid_latent: bfloat16 [65536, 512], P(('mesh', 'band')), may hold values from -6 to 6
- weights: bfloat16 [9, 512, 512], replicated, may hold values from -0.25 to 0.25
- biases: float32 [3, 512], replicated, may hold values from -4 to 4
- gains: float32 [3, 512], replicated, may hold values from 0.5 to 2
- cotangent: bfloat16 [65536, 512], P(('mesh', 'band')), may hold values from -6 to 6
- halo_index: int32 [128, 3, 128], P(('mesh', 'band')), may hold values from 0 to 511
- edge_source: int32 [128, 3, 8, 128], P(('mesh', 'band')), may hold values from 0 to 511
- edge_target: int32 [128, 3, 8, 128], P(('mesh', 'band')), may hold values from 0 to 511
- block_count: int32 [128, 3], P(('mesh', 'band')), may hold values from 1 to 8, as said below
- decoder_send: int32 [128, 128, 8], P(('mesh', 'band')), may hold values from 0 to 511
- decoder_source: int32 [3, 65536], P(None, ('mesh', 'band')), may hold values from 0 to 1023, as said below
Outputs:
- grad_mesh: bfloat16 [65536, 512], P(('mesh', 'band'))
- grad_grid: bfloat16 [65536, 512], P(('mesh', 'band'))
- grad_weights: float32 [9, 512, 512], replicated
- grad_biases: float32 [3, 512], replicated
- grad_gains: float32 [3, 512], replicated
The draws below stay inside these ranges and needn't reach their ends.
Inputs may be any that keep to these rules, and one draw needn't show every extreme that they name: `block_count`: every entry is 1 to 8, and 8 is reached on some block in every draw. `edge_source`: blocks at or past block_count hold valid indices but carry no edge. `decoder_source`: each device's columns index that device's 1024 received rows; each of those rows is read by at least one edge.
All inputs are finite; a program needn't handle non-finite values.
Results may differ from the reference program's by a relative error of at most 0.025.
Values may be sent and summed in bfloat16 or wider, within the bound.
No kernel may reach another device: no remote copies, remote signals or barrier semaphores. Data moves between devices by JAX's collectives and lax.ppermute only.
A program may use at most 128 MiB of HBM per device.

```python
import math
import jax
import jax.numpy as jnp
from jax import lax

D = 512
MN = 512
GN = 512
HALO = 128
NB = 8
EB = 128
DSLOT = 8
SHARDS = 128
SLOTS = 1024
NM = 65536
NG = 65536
N_MESH = 32
N_BAND = 4


def draw_block_count(key, part):
    key = jax.random.fold_in(key, 11)
    first_key, second_key, third_key = jax.random.split(key, 3)
    larger = jnp.maximum(jax.random.randint(first_key, (SHARDS, 3), 1, NB + 1, dtype=jnp.int32), jax.random.randint(second_key, (SHARDS, 3), 1, NB + 1, dtype=jnp.int32))
    chosen = jax.random.randint(third_key, (), 0, SHARDS * 3, dtype=jnp.int32)
    flattened = jnp.where(jnp.arange(SHARDS * 3, dtype=jnp.int32) == chosen, NB, larger.reshape(-1))
    return flattened.reshape(SHARDS, 3).astype(jnp.int32)


def draw_decoder_source(key, part):
    key = jax.random.fold_in(key, 23)

    def one_device(device_key):
        first_key, second_key = jax.random.split(device_key)
        additional = jax.random.randint(first_key, (3 * GN - SLOTS,), 0, SLOTS, dtype=jnp.int32)
        joined = jnp.concatenate([jnp.arange(SLOTS, dtype=jnp.int32), additional])
        return jax.random.permutation(second_key, joined)
    columns = jax.vmap(one_device)(jax.random.split(key, SHARDS))
    return columns.reshape(SHARDS, 3, GN).transpose(1, 0, 2).reshape(3, SHARDS * GN).astype(jnp.int32)


def touch_ends(drawn, key, low, high):
    longest = drawn.shape.index(max(drawn.shape))
    spots = []
    for shift in (0, 1):
        where = [jax.random.randint(jax.random.fold_in(key, axis), (), 0, length) for axis, length in enumerate(drawn.shape)]
        where[longest] = (where[longest] + shift) % drawn.shape[longest]
        spots.append(tuple(where))
    return drawn.at[spots[0]].set(low).at[spots[1]].set(high)


def block_levels(key, extent, cuts, low, largest):
    def one(dim, blocks):
        steps = jax.random.uniform(jax.random.fold_in(jax.random.fold_in(key, 6), dim), (blocks,), jnp.float32, low / len(cuts), largest / len(cuts))
        return jnp.repeat(jnp.exp(steps), extent[dim] // blocks).reshape((-1,) + (1,) * (len(extent) - dim - 1))

    loudness = one(*cuts[0])
    for cut in cuts[1:]:
        loudness = loudness * one(*cut)
    return loudness


def scatter_about(key, dims, spread, bound, cuts=(), kind=jnp.bfloat16):
    level = block_levels(key, dims, cuts, -0.22, 0.18) if cuts else 1.0
    drawn = jax.random.normal(key, dims, jnp.float32) * spread * level
    return jnp.minimum(jnp.maximum(drawn, -bound), bound).astype(kind)


def setup_inputs(seed: int = 0) -> dict:
    splits = jax.random.split(jax.random.key(seed), 13)
    mesh_latent = scatter_about(splits[0], (NM, D), 1.0, 6.0, ((0, 128),))
    grid_latent = scatter_about(splits[1], (NG, D), 1.0, 6.0, ((0, 128),))
    weights = scatter_about(splits[2], (9, D, D), D ** -0.5, 0.25)
    biases = scatter_about(splits[3], (3, D), 0.7, 4.0, (), jnp.float32)
    gains = jnp.clip(jnp.exp(jax.random.uniform(splits[4], (3, D), jnp.float32, math.log(0.5), math.log(2.0))), 0.5, 2.0)
    cotangent = scatter_about(splits[5], (NG, D), 1.0, 6.0, ((0, 128),))
    halo_index = touch_ends(jax.random.randint(splits[6], (SHARDS, 3, HALO), 0, MN), jax.random.fold_in(splits[6], 1), 0, MN - 1).astype(jnp.int32)
    edge_source = touch_ends(jax.random.randint(splits[7], (SHARDS, 3, NB, EB), 0, N_BAND * HALO), jax.random.fold_in(splits[7], 1), 0, (N_BAND * HALO) - 1).astype(jnp.int32)
    edge_target = touch_ends(jax.random.randint(splits[8], (SHARDS, 3, NB, EB), 0, MN), jax.random.fold_in(splits[8], 1), 0, MN - 1).astype(jnp.int32)
    block_count = draw_block_count(jax.random.fold_in(splits[12], 71), 0)
    decoder_send = touch_ends(jax.random.randint(splits[10], (SHARDS, SHARDS, DSLOT), 0, MN), jax.random.fold_in(splits[10], 1), 0, MN - 1).astype(jnp.int32)
    decoder_source = draw_decoder_source(jax.random.fold_in(splits[12], 71), 0)
    return dict(mesh_latent=mesh_latent, grid_latent=grid_latent, weights=weights, biases=biases, gains=gains, cotangent=cotangent, halo_index=halo_index, edge_source=edge_source, edge_target=edge_target, block_count=block_count, decoder_send=decoder_send, decoder_source=decoder_source)


EPSILON = 1e-05

def matmul(left, right):
    return jnp.dot(left, right, preferred_element_type=jnp.float32)

def times_transpose(left, right):
    return lax.dot_general(left, right, (((1,), (1,)), ((), ())), preferred_element_type=jnp.float32)

def outer_sum(left, right):
    return lax.dot_general(left, right, (((0,), (0,)), ((), ())), preferred_element_type=jnp.float32)

def silu_slope(preact):
    sigmoid_value = jax.nn.sigmoid(preact)
    return sigmoid_value * (1.0 + preact * (1.0 - sigmoid_value))

def norm_forward(mixed):
    average = lax.optimization_barrier(jnp.mean(mixed, axis=-1, keepdims=True))
    centered = mixed - average
    inverse = lax.rsqrt(lax.optimization_barrier(jnp.mean(centered * centered, axis=-1, keepdims=True)) + EPSILON)
    return (centered * inverse, inverse)

def norm_backward(normed, inverse, gain, upstream):
    scaled = upstream * gain
    grad_input = inverse * (scaled - lax.optimization_barrier(jnp.mean(scaled, axis=-1, keepdims=True)) - normed * lax.optimization_barrier(jnp.mean(scaled * normed, axis=-1, keepdims=True)))
    gain_grad = lax.optimization_barrier(jnp.sum(upstream * normed, axis=0))
    return (grad_input, gain_grad)

def edge_core(preact, weight_out):
    hidden = jax.nn.silu(preact).astype(jnp.bfloat16)
    normed, inverse = norm_forward(matmul(hidden, weight_out))
    return (hidden, normed, inverse)

def edge_backward(preact, hidden, normed, inverse, weight_out, gain, upstream):
    grad_mixed, gain_grad = norm_backward(normed, inverse, gain, upstream)
    grad_mixed = grad_mixed.astype(jnp.bfloat16)
    grad_pre = (times_transpose(grad_mixed, weight_out) * silu_slope(preact)).astype(jnp.bfloat16)
    return (grad_pre, outer_sum(hidden, grad_mixed), gain_grad)

def pick_rows(table_rows, row_index):
    return table_rows[row_index]

def scatter_rows(values, row_index):
    return jnp.zeros((MN, D), jnp.float32).at[row_index].add(values.astype(jnp.float32))

def reference(mesh_latent, grid_latent, weights, biases, gains, cotangent, halo_index, edge_source, edge_target, block_count, decoder_send, decoder_source):
    shards = N_MESH * N_BAND
    group_rows = N_BAND * HALO
    src_proj = matmul(mesh_latent, weights[0]).astype(jnp.bfloat16)
    dst_proj = (matmul(mesh_latent, weights[1]) + biases[0]).astype(jnp.bfloat16)
    outgoing = jax.vmap(pick_rows)(src_proj.reshape(shards, MN, D), halo_index)
    outgoing = outgoing.reshape(N_MESH, N_BAND, 3, HALO, D)
    tables = jnp.stack([jnp.roll(outgoing[:, :, group], group - 1, axis=0).reshape(N_MESH, group_rows, D) for group in range(3)], axis=1).reshape(N_MESH, 3 * group_rows, D)
    offsets = (jnp.arange(3, dtype=jnp.int32) * group_rows)[None, :, None, None]
    sources = (edge_source + offsets).reshape(shards, -1)
    targets = edge_target.reshape(shards, -1)
    live = jnp.arange(NB, dtype=jnp.int32)[None, None, :, None] < block_count[:, :, None, None]
    live = jnp.broadcast_to(live, edge_source.shape).reshape(shards, -1).astype(jnp.float32)
    dst_blocks = dst_proj.reshape(shards, MN, D)
    devices = jnp.arange(shards, dtype=jnp.int32)

    def edge_activations(device, source_index, target_index):
        table = tables[device // N_BAND]
        preact = table[source_index].astype(jnp.float32) + dst_blocks[device][target_index].astype(jnp.float32)
        hidden, normed, inverse = edge_core(preact, weights[2])
        return (preact, hidden, normed, inverse)

    def aggregate_block(inputs):
        device, source_index, target_index, live_edge = inputs
        preact, hidden, normed, inverse = edge_activations(device, source_index, target_index)
        messages = normed * gains[0] * live_edge[:, None]
        return jnp.zeros((MN, D), jnp.float32).at[target_index].add(messages).astype(jnp.bfloat16)
    aggregate = lax.map(aggregate_block, (devices, sources, targets, live)).reshape(-1, D)
    node_pre = matmul(mesh_latent, weights[3]) + matmul(aggregate, weights[4]) + biases[1]
    node_hidden = jax.nn.silu(node_pre).astype(jnp.bfloat16)
    node_normed, node_inverse = norm_forward(matmul(node_hidden, weights[5]))
    new_mesh = (mesh_latent.astype(jnp.float32) + node_normed * gains[1]).astype(jnp.bfloat16)
    mesh_value = matmul(new_mesh, weights[6]).astype(jnp.bfloat16)
    outbound = jax.vmap(pick_rows)(mesh_value.reshape(shards, MN, D), decoder_send)
    received = jnp.swapaxes(outbound, 0, 1).reshape(shards, shards * DSLOT, D)
    grid_proj = (matmul(grid_latent, weights[7]) + biases[2]).astype(jnp.bfloat16).reshape(shards, GN, D)
    dec_index = decoder_source.reshape(3, shards, GN).transpose(1, 0, 2).reshape(shards, 3 * GN)
    cot_blocks = cotangent.reshape(shards, GN, D)

    def decoder_block(carry, inputs):
        table, projected, upstream_rows, source_index = inputs
        dec_pre = (table[source_index].astype(jnp.float32).reshape(3, GN, D) + projected.astype(jnp.float32)).reshape(-1, D)
        dec_hidden, dec_normed, dec_inverse = edge_core(dec_pre, weights[8])
        upstream = jnp.broadcast_to(upstream_rows.astype(jnp.float32), (3, GN, D)).reshape(-1, D)
        grad_pre, weight_grad, gain_grad = edge_backward(dec_pre, dec_hidden, dec_normed, dec_inverse, weights[8], gains[2], upstream)
        proj_grad = lax.optimization_barrier(jnp.sum(grad_pre.astype(jnp.float32).reshape(3, GN, D), axis=0)).astype(jnp.bfloat16)
        slot_grad = jnp.zeros((shards * DSLOT, D), jnp.float32).at[source_index].add(grad_pre.astype(jnp.float32)).astype(jnp.bfloat16)
        return ((carry[0] + weight_grad, carry[1] + gain_grad), (proj_grad, slot_grad))
    start = (jnp.zeros((D, D), jnp.float32), jnp.zeros((D,), jnp.float32))
    (dec_weight_grad, dec_gain_grad), (grid_grad_proj, slot_grad) = lax.scan(decoder_block, start, (received, grid_proj, cot_blocks, dec_index))
    grid_grad_proj = grid_grad_proj.reshape(-1, D)
    grad_grid = (cotangent.astype(jnp.float32) + times_transpose(grid_grad_proj, weights[7])).astype(jnp.bfloat16)
    returned = jnp.swapaxes(slot_grad.reshape(shards, shards, DSLOT, D), 0, 1).reshape(shards, -1, D)
    mesh_value_grad = jax.vmap(scatter_rows)(returned, decoder_send.reshape(shards, -1))
    mesh_value_grad = mesh_value_grad.astype(jnp.bfloat16).reshape(-1, D)
    new_mesh_grad = times_transpose(mesh_value_grad, weights[6])
    node_grad_out, node_gain_grad = norm_backward(node_normed, node_inverse, gains[1], new_mesh_grad)
    node_grad_out = node_grad_out.astype(jnp.bfloat16)
    node_grad_pre = (times_transpose(node_grad_out, weights[5]) * silu_slope(node_pre)).astype(jnp.bfloat16)
    aggregate_grad = times_transpose(node_grad_pre, weights[4]).astype(jnp.bfloat16)
    agg_blocks = aggregate_grad.reshape(shards, MN, D)

    def edge_block(carry, inputs):
        device, source_index, target_index, live_edge = inputs
        preact, hidden, normed, inverse = edge_activations(device, source_index, target_index)
        upstream = agg_blocks[device][target_index].astype(jnp.float32) * live_edge[:, None]
        grad_pre, weight_grad, gain_grad = edge_backward(preact, hidden, normed, inverse, weights[2], gains[0], upstream)
        grad_wide = grad_pre.astype(jnp.float32)
        dst_part = jnp.zeros((MN, D), jnp.float32).at[target_index].add(grad_wide).astype(jnp.bfloat16)
        table_part = jnp.zeros((3 * group_rows, D), jnp.float32).at[source_index].add(grad_wide).astype(jnp.bfloat16)
        return ((carry[0] + weight_grad, carry[1] + gain_grad), (dst_part, table_part))
    (edge_weight_grad, edge_gain_grad), (dst_grad, table_grad) = lax.scan(edge_block, start, (devices, sources, targets, live))
    dst_grad = dst_grad.reshape(-1, D)
    table_grad = table_grad.astype(jnp.float32).reshape(N_MESH, N_BAND, 3, N_BAND, HALO, D)
    halo_grad = jnp.stack([lax.optimization_barrier(jnp.sum(jnp.roll(table_grad[:, :, group], 1 - group, axis=0), axis=1)) for group in range(3)], axis=2).reshape(shards, 3 * HALO, D)
    src_grad = jax.vmap(scatter_rows)(halo_grad, halo_index.reshape(shards, -1))
    src_grad = src_grad.astype(jnp.bfloat16).reshape(-1, D)
    grad_mesh = (new_mesh_grad + times_transpose(node_grad_pre, weights[3]) + times_transpose(dst_grad, weights[1]) + times_transpose(src_grad, weights[0])).astype(jnp.bfloat16)
    factor = 1.0 / math.sqrt(GN * shards)
    grad_weights = jnp.stack([outer_sum(mesh_latent, src_grad), outer_sum(mesh_latent, dst_grad), edge_weight_grad, outer_sum(mesh_latent, node_grad_pre), outer_sum(aggregate, node_grad_pre), outer_sum(node_hidden, node_grad_out), outer_sum(new_mesh, mesh_value_grad), outer_sum(grid_latent, grid_grad_proj), dec_weight_grad]) * factor
    grad_biases = jnp.stack([lax.optimization_barrier(jnp.sum(dst_grad.astype(jnp.float32), axis=0)), lax.optimization_barrier(jnp.sum(node_grad_pre.astype(jnp.float32), axis=0)), lax.optimization_barrier(jnp.sum(grid_grad_proj.astype(jnp.float32), axis=0))]) * factor
    grad_gains = jnp.stack([edge_gain_grad, node_gain_grad, dec_gain_grad]) * factor
    return (grad_mesh, grad_grid, grad_weights, grad_biases, grad_gains)
```

```python
import functools
import math

import jax
import jax.numpy as jnp
from jax import lax
from jax.experimental import pallas as pl
from jax.experimental.pallas import tpu as pltpu
from jax.sharding import PartitionSpec as P

EPSILON = 1e-05
BF = jnp.bfloat16
F32 = jnp.float32
LANES = 128
BOTH = ("mesh", "band")


def dot(left, right):
    return jnp.dot(left, right, preferred_element_type=F32)


def dot_t(left, right):
    return lax.dot_general(left, right, (((1,), (1,)), ((), ())), preferred_element_type=F32)


def t_dot(left, right):
    return lax.dot_general(left, right, (((0,), (0,)), ((), ())), preferred_element_type=F32)


def sigmoid(value):
    return 0.5 * jnp.tanh(0.5 * value) + 0.5


def row_mean(value):
    return jnp.mean(value, axis=-1, keepdims=True)


def norm_forward(mixed):
    centered = mixed - row_mean(mixed)
    inverse = lax.rsqrt(row_mean(centered * centered) + EPSILON)
    return centered * inverse, inverse


def norm_backward(normed, inverse, scaled):
    return inverse * (scaled - row_mean(scaled) - normed * row_mean(scaled * normed))


def one_hot(mask):
    return jnp.where(mask, 1.0, 0.0).astype(BF)


def as_columns(index):
    return jnp.transpose(index.astype(F32)).astype(jnp.int32)


def pick_matrix(columns, first, blocks, size):
    lanes = lax.broadcasted_iota(jnp.int32, (LANES, size), 1)
    parts = [one_hot(columns[:, b : b + 1] == lanes) for b in range(first, first + blocks)]
    return jnp.concatenate(parts, axis=0)


def place_matrix(rows, first, blocks, size):
    sublanes = lax.broadcasted_iota(jnp.int32, (size, LANES), 0)
    parts = [one_hot(rows[b : b + 1, :] == sublanes) for b in range(first, first + blocks)]
    return jnp.concatenate(parts, axis=1)


def call(kernel, outs, args, flops, scratch=()):
    moved = sum(a.size * a.dtype.itemsize for a in args)
    moved += sum(math.prod(s) * jnp.dtype(t).itemsize for s, t in outs)
    return pl.pallas_call(
        kernel,
        out_shape=[jax.ShapeDtypeStruct(s, t) for s, t in outs],
        in_specs=[pl.BlockSpec(memory_space=pltpu.VMEM)] * len(args),
        out_specs=[pl.BlockSpec(memory_space=pltpu.VMEM)] * len(outs),
        scratch_shapes=list(scratch),
        compiler_params=pltpu.CompilerParams(vmem_limit_bytes=56 * 1024 * 1024),
        cost_estimate=pl.CostEstimate(flops=flops, bytes_accessed=moved, transcendentals=0),
    )(*args)


def halo_kernel(mesh_ref, index_ref, out_ref):
    columns = as_columns(index_ref[...])
    for c in range(3):
        out_ref[c] = dot(pick_matrix(columns, c, 1, mesh_ref.shape[0]), mesh_ref[...]).astype(BF)


def local_kernel(mesh_ref, grid_ref, w1, w3, w7, biases, dst_ref, part_ref, proj_ref):
    mesh = mesh_ref[...]
    dst_ref[...] = (dot(mesh, w1[...]) + biases[0:1, :]).astype(BF)
    part_ref[...] = dot(mesh, w3[...]) + biases[1:2, :]
    proj_ref[...] = (dot(grid_ref[...], w7[...]) + biases[2:3, :]).astype(BF)


def edge_forward_kernel(*refs):
    tables = refs[:12]
    (dst_ref, source_ref, target_ref, w0, w2, w4, w5, w6, mesh_ref, part_ref, gains, send_ref) = refs[12:24]
    (
        hidden_ref, slope_ref, normed_ref, inverse_ref, summed_ref, aggregate_ref, node_hidden_ref,
        node_slope_ref, node_normed_ref, node_inverse_ref, new_mesh_ref, outbound_ref,
    ) = refs[24:36]
    table_ref = refs[36]
    features = dst_ref.shape[1]
    mesh_rows = dst_ref.shape[0]
    for c in range(3):
        for j in range(4):
            table_ref[c, j * LANES : (j + 1) * LANES, :] = dot(tables[4 * c + j][...], w0[...]).astype(BF)
    summed_ref[...] = jnp.zeros_like(summed_ref)

    def group(c, carry):
        source_columns = as_columns(source_ref[c])
        target_columns = as_columns(target_ref[c])
        targets = target_ref[c]
        table = table_ref[c]
        for half in range(2):
            preact = dot(pick_matrix(source_columns, 4 * half, 4, 4 * LANES), table)
            preact += dot(pick_matrix(target_columns, 4 * half, 4, mesh_rows), dst_ref[...])
            gate = sigmoid(preact)
            hidden = (preact * gate).astype(BF)
            normed, inverse = norm_forward(dot(hidden, w2[...]))
            normed = normed.astype(BF)
            rows = pl.ds(pl.multiple_of(c * 8 * LANES + half * 4 * LANES, 4 * LANES), 4 * LANES)
            hidden_ref[rows, :] = hidden
            slope_ref[rows, :] = (gate * (1.0 + preact * (1.0 - gate))).astype(BF)
            normed_ref[rows, :] = normed
            inverse_ref[rows, :] = inverse
            summed_ref[...] += dot(place_matrix(targets, 4 * half, 4, mesh_rows), normed)
        return carry

    lax.fori_loop(0, 3, group, 0)
    aggregate = (summed_ref[...] * gains[0:1, :]).astype(BF)
    aggregate_ref[...] = aggregate
    node_pre = part_ref[...] + dot(aggregate, w4[...])
    gate = sigmoid(node_pre)
    node_hidden = (node_pre * gate).astype(BF)
    node_hidden_ref[...] = node_hidden
    node_slope_ref[...] = gate * (1.0 + node_pre * (1.0 - gate))
    normed, inverse = norm_forward(dot(node_hidden, w5[...]))
    node_normed_ref[...] = normed
    node_inverse_ref[...] = inverse
    new_mesh = (mesh_ref[...].astype(F32) + normed * gains[1:2, :]).astype(BF)
    new_mesh_ref[...] = new_mesh
    value = dot(new_mesh, w6[...]).astype(BF)
    columns = as_columns(send_ref[...])
    for half in range(2):
        outbound_ref[half * 4 * LANES : (half + 1) * 4 * LANES, :] = dot(
            pick_matrix(columns, 4 * half, 4, mesh_rows), value
        ).astype(BF)


def decoder_kernel(
    received_ref, proj_ref, cot_ref, source_ref, w8, gains,
    slot_ref, proj_grad_ref, weight_ref, gain_ref, slot_sum, proj_sum,
):
    slots = received_ref.shape[0]
    columns = as_columns(source_ref[...])
    sources = source_ref[...]
    cot = cot_ref[...].astype(F32)
    scaled = cot * gains[2:3, :]
    scaled_mean = row_mean(scaled)
    for c in range(3):
        preact = dot(pick_matrix(columns, 4 * c, 4, slots), received_ref[...]) + proj_ref[...].astype(F32)
        gate = sigmoid(preact)
        hidden = (preact * gate).astype(BF)
        slope = gate * (1.0 + preact * (1.0 - gate))
        normed, inverse = norm_forward(dot(hidden, w8[...]))
        grad_mixed = (inverse * (scaled - scaled_mean - normed * row_mean(scaled * normed))).astype(BF)
        gain = jnp.sum(cot * normed, axis=0, keepdims=True)
        weight = t_dot(hidden, grad_mixed)
        grad_pre = (dot_t(grad_mixed, w8[...]) * slope).astype(BF)
        placed = dot(place_matrix(sources, 4 * c, 4, slots), grad_pre)
        if c == 0:
            gain_ref[...] = gain
            weight_ref[...] = weight
            slot_sum[...] = placed
            proj_sum[...] = grad_pre.astype(F32)
        else:
            gain_ref[...] += gain
            weight_ref[...] += weight
            slot_sum[...] += placed
            proj_sum[...] += grad_pre.astype(F32)
    slot_ref[...] = slot_sum[...].astype(BF)
    proj_grad_ref[...] = proj_sum[...].astype(BF)


def grid_kernel(factor, proj_grad_ref, cot_ref, grid_ref, w7, dec_weight, grad_ref, weights_ref, bias_ref):
    proj_grad = proj_grad_ref[...]
    grad_ref[...] = (cot_ref[...].astype(F32) + dot_t(proj_grad, w7[...])).astype(BF)
    weights_ref[0] = (t_dot(grid_ref[...], proj_grad) * factor).astype(BF)
    weights_ref[1] = (dec_weight[...] * factor).astype(BF)
    bias_ref[...] = jnp.sum(proj_grad.astype(F32), axis=0, keepdims=True)


def node_backward_kernel(
    returned_ref, send_ref, w6, w5, w4, node_normed_ref, node_inverse_ref, node_slope_ref, summed_ref, gains,
    value_grad_ref, new_grad_ref, out_grad_ref, pre_grad_ref, scaled_ref, gain_ref,
):
    mesh_rows = node_normed_ref.shape[0]
    value_grad = dot(place_matrix(send_ref[...], 0, 8, mesh_rows), returned_ref[...]).astype(BF)
    value_grad_ref[...] = value_grad
    new_grad = dot_t(value_grad, w6[...])
    new_grad_ref[...] = new_grad
    normed = node_normed_ref[...]
    out_grad = norm_backward(normed, node_inverse_ref[...], new_grad * gains[1:2, :]).astype(BF)
    out_grad_ref[...] = out_grad
    pre_grad = (dot_t(out_grad, w5[...]) * node_slope_ref[...]).astype(BF)
    pre_grad_ref[...] = pre_grad
    aggregate_grad = dot_t(pre_grad, w4[...])
    scaled_ref[...] = (aggregate_grad * gains[0:1, :]).astype(BF)
    gain_ref[0:1, :] = jnp.sum(aggregate_grad * summed_ref[...], axis=0, keepdims=True)
    gain_ref[1:2, :] = jnp.sum(new_grad * normed, axis=0, keepdims=True)


def node_weights_kernel(
    factor, mesh_ref, aggregate_ref, node_hidden_ref, new_mesh_ref, pre_grad_ref, out_grad_ref, value_grad_ref,
    weights_ref,
):
    pre_grad = pre_grad_ref[...]
    weights_ref[0] = (t_dot(mesh_ref[...], pre_grad) * factor).astype(BF)
    weights_ref[1] = (t_dot(aggregate_ref[...], pre_grad) * factor).astype(BF)
    weights_ref[2] = (t_dot(node_hidden_ref[...], out_grad_ref[...]) * factor).astype(BF)
    weights_ref[3] = (t_dot(new_mesh_ref[...], value_grad_ref[...]) * factor).astype(BF)


def edge_backward_kernel(
    scaled_ref, source_ref, target_ref, w2, hidden_ref, slope_ref, normed_ref, inverse_ref,
    table_ref, dst_ref, weight_ref, table_sum, dst_sum,
):
    mesh_rows = scaled_ref.shape[0]
    dst_sum[...] = jnp.zeros_like(dst_sum)
    weight_ref[...] = jnp.zeros_like(weight_ref)

    def group(c, carry):
        target_columns = as_columns(target_ref[c])
        targets = target_ref[c]
        sources = source_ref[c]
        for half in range(2):
            rows = pl.ds(pl.multiple_of(c * 8 * LANES + half * 4 * LANES, 4 * LANES), 4 * LANES)
            scaled = dot(pick_matrix(target_columns, 4 * half, 4, mesh_rows), scaled_ref[...])
            grad_mixed = norm_backward(normed_ref[rows, :].astype(F32), inverse_ref[rows, :], scaled).astype(BF)
            weight_ref[...] += t_dot(hidden_ref[rows, :], grad_mixed)
            grad_pre = (dot_t(grad_mixed, w2[...]) * slope_ref[rows, :].astype(F32)).astype(BF)
            dst_sum[...] += dot(place_matrix(targets, 4 * half, 4, mesh_rows), grad_pre)
            placed = dot(place_matrix(sources, 4 * half, 4, 4 * LANES), grad_pre)
            if half == 0:
                table_sum[...] = placed
            else:
                table_ref[c] = (table_sum[...] + placed).astype(BF)
        return carry

    lax.fori_loop(0, 3, group, 0)
    dst_ref[...] = dst_sum[...].astype(BF)


def edge_weights_kernel(factor, *refs):
    tables = refs[:12]
    (
        table_grad_ref, mesh_ref, dst_grad_ref, edge_weight, new_grad_ref, pre_grad_ref, w1, w3,
        gains_ref, dec_gain_ref, grid_bias_ref, partial_ref, weights_ref,
    ) = refs[12:]
    total = None
    for c in range(3):
        for j in range(4):
            part = t_dot(tables[4 * c + j][...], table_grad_ref[c, j * LANES : (j + 1) * LANES, :])
            total = part if total is None else total + part
    size = mesh_ref.shape[1]
    weights_ref[0:size, :] = (total * factor).astype(BF)
    dst_grad = dst_grad_ref[...]
    pre_grad = pre_grad_ref[...]
    weights_ref[size : 2 * size, :] = (t_dot(mesh_ref[...], dst_grad) * factor).astype(BF)
    weights_ref[2 * size : 3 * size, :] = (edge_weight[...] * factor).astype(BF)
    small = jnp.concatenate(
        [
            jnp.sum(dst_grad.astype(F32), axis=0, keepdims=True),
            jnp.sum(pre_grad.astype(F32), axis=0, keepdims=True),
            grid_bias_ref[...],
            gains_ref[...],
            dec_gain_ref[...],
            jnp.zeros((10, size), F32),
        ],
        axis=0,
    )
    weights_ref[3 * size :, :] = (small * factor).astype(BF)
    partial_ref[...] = new_grad_ref[...] + dot_t(pre_grad, w3[...]) + dot_t(dst_grad, w1[...])


def final_kernel(*refs):
    parts = refs[:12]
    index_ref, partial_ref, w0, grad_ref = refs[12:]
    mesh_rows = partial_ref.shape[0]
    src_grad = None
    for c in range(3):
        halo = parts[4 * c][...].astype(F32)
        for j in range(1, 4):
            halo += parts[4 * c + j][...].astype(F32)
        part = dot(place_matrix(index_ref[...], c, 1, mesh_rows), halo.astype(BF))
        src_grad = part if src_grad is None else src_grad + part
    grad_ref[...] = (partial_ref[...] + dot_t(src_grad.astype(BF), w0[...])).astype(BF)


def routes(n_mesh, n_band):
    found = {}
    for c in range(3):
        for step in range(n_band):
            if c == 1 and step == 0:
                continue
            found[c, step] = [
                (((i - c + 1) % n_mesh) * n_band + (j + step) % n_band, i * n_band + j)
                for i in range(n_mesh)
                for j in range(n_band)
            ]
    return found


def pad_rows(index, rows):
    return jnp.pad(index, ((0, rows - index.shape[0]), (0, 0)))


def body(
    mesh_latent, grid_latent, weights, biases, gains, cotangent, halo_index, edge_source, edge_target,
    block_count, decoder_send, decoder_source,
):
    n_mesh, n_band = lax.axis_size("mesh"), lax.axis_size("band")
    mesh_rows, features = mesh_latent.shape
    grid_rows = grid_latent.shape[0]
    shards, slots_each = decoder_send.shape[1:]
    slots = shards * slots_each
    blocks, block = edge_source.shape[2:]
    edges = 3 * blocks * block
    square = 2 * features * features
    factor = 1.0 / math.sqrt(grid_rows * n_mesh * n_band)
    w = [weights[k] for k in range(9)]
    paths = routes(n_mesh, n_band)

    halo_rows = pad_rows(halo_index[0], 8)
    (outgoing,) = call(halo_kernel, [((3, LANES, features), BF)], [mesh_latent, halo_rows], 384 * square)
    tables = []
    for c in range(3):
        for step in range(n_band):
            tables.append(lax.ppermute(outgoing[c], BOTH, paths[c, step]) if (c, step) in paths else outgoing[c])

    band = lax.axis_index("band")
    sources = (edge_source[0] - band * LANES) & (n_band * LANES - 1)
    live = jnp.arange(blocks, dtype=jnp.int32)[None, :, None] < block_count[0][:, None, None]
    targets = jnp.where(live, edge_target[0], -1)
    send_rows = decoder_send[0].reshape(slots // LANES, LANES)
    source_rows = pad_rows(decoder_source.reshape(3 * grid_rows // LANES, LANES), 16)

    dst_proj, node_part, grid_proj = call(
        local_kernel,
        [((mesh_rows, features), BF), ((mesh_rows, features), F32), ((grid_rows, features), BF)],
        [mesh_latent, grid_latent, w[1], w[3], w[7], biases],
        3 * mesh_rows * square,
    )
    wide, wide32 = ((mesh_rows, features), BF), ((mesh_rows, features), F32)
    (
        hidden, slope, normed, inverse, summed, aggregate, node_hidden, node_slope, node_normed, node_inverse,
        new_mesh, outbound,
    ) = call(
        edge_forward_kernel,
        [
            ((edges, features), BF), ((edges, features), BF), ((edges, features), BF), ((edges, 1), F32),
            wide32, wide, wide, wide32, wide32, ((mesh_rows, 1), F32), wide, ((slots, features), BF),
        ],
        tables + [dst_proj, sources, targets, w[0], w[2], w[4], w[5], w[6], mesh_latent, node_part, gains, send_rows],
        5 * edges * square,
        [pltpu.VMEM((3, n_band * LANES, features), BF)],
    )
    received = lax.all_to_all(
        outbound.reshape(shards, slots_each, features), BOTH, split_axis=0, concat_axis=0, tiled=True
    ).reshape(slots, features)
    slot_grad, proj_grad, dec_weight, dec_gain = call(
        decoder_kernel,
        [((slots, features), BF), ((grid_rows, features), BF), ((features, features), F32), ((1, features), F32)],
        [received, grid_proj, cotangent, source_rows, w[8], gains],
        7 * 3 * grid_rows * square,
        [pltpu.VMEM((slots, features), F32), pltpu.VMEM((grid_rows, features), F32)],
    )
    returned = lax.all_to_all(
        slot_grad.reshape(shards, slots_each, features), BOTH, split_axis=0, concat_axis=0, tiled=True
    ).reshape(slots, features)
    grad_grid, late_weights, grid_bias = call(
        functools.partial(grid_kernel, factor),
        [((grid_rows, features), BF), ((2, features, features), BF), ((1, features), F32)],
        [proj_grad, cotangent, grid_latent, w[7], dec_weight],
        2 * grid_rows * square,
    )
    late_weights = lax.psum(late_weights, BOTH)

    value_grad, new_grad, out_grad, pre_grad, scaled, node_gains = call(
        node_backward_kernel,
        [wide, wide32, wide, wide, wide, ((2, features), F32)],
        [returned, send_rows, w[6], w[5], w[4], node_normed, node_inverse, node_slope, summed, gains],
        5 * mesh_rows * square,
    )
    (node_weights,) = call(
        functools.partial(node_weights_kernel, factor),
        [((4, features, features), BF)],
        [mesh_latent, aggregate, node_hidden, new_mesh, pre_grad, out_grad, value_grad],
        4 * mesh_rows * square,
    )
    node_weights = lax.psum(node_weights, BOTH)
    table_grad, dst_grad, edge_weight = call(
        edge_backward_kernel,
        [((3, n_band * LANES, features), BF), wide, ((features, features), F32)],
        [scaled, sources, targets, w[2], hidden, slope, normed, inverse],
        5 * edges * square,
        [pltpu.VMEM((n_band * LANES, features), F32), pltpu.VMEM((mesh_rows, features), F32)],
    )
    parts = []
    for c in range(3):
        for step in range(n_band):
            sent = table_grad[c, step * LANES : (step + 1) * LANES]
            if (c, step) in paths:
                sent = lax.ppermute(sent, BOTH, [(b, a) for a, b in paths[c, step]])
            parts.append(sent)
    partial, edge_weights = call(
        functools.partial(edge_weights_kernel, factor),
        [wide32, ((3 * features + 16, features), BF)],
        tables
        + [table_grad, mesh_latent, dst_grad, edge_weight, new_grad, pre_grad, w[1], w[3], node_gains, dec_gain, grid_bias],
        6 * mesh_rows * square,
    )
    edge_weights = lax.psum(edge_weights, BOTH)
    (grad_mesh,) = call(
        final_kernel, [wide], parts + [halo_rows, partial, w[0]], 2 * mesh_rows * square
    )
    grad_weights = jnp.concatenate(
        [
            edge_weights[: 3 * features].reshape(3, features, features).astype(F32),
            node_weights.astype(F32),
            late_weights.astype(F32),
        ],
        axis=0,
    )
    small = edge_weights[3 * features :].astype(F32)
    return grad_mesh, grad_grid, grad_weights, small[0:3], small[3:6]


def solution(mesh):
    both = P(BOTH)
    return jax.shard_map(
        body,
        mesh=mesh,
        in_specs=(both, both, P(), P(), P(), both, both, both, both, both, both, P(None, BOTH)),
        out_specs=(both, both, P(), P(), P()),
        check_vma=False,
    )
```

```python
import functools
import math

import jax
import jax.numpy as jnp
from jax import lax
from jax.experimental import pallas as pl
from jax.experimental.pallas import tpu as pltpu
from jax.sharding import PartitionSpec as P

EPSILON = 1e-05
BF = jnp.bfloat16
F32 = jnp.float32
LANES = 128
TILE = 16
PIECES = 64
AXES = ("x", "y", "core", "z")
CHIPS = ("x", "y", "z")


def dot(left, right):
    return jnp.dot(left, right, preferred_element_type=F32)


def dot_t(left, right):
    return lax.dot_general(left, right, (((1,), (1,)), ((), ())), preferred_element_type=F32)


def t_dot(left, right):
    return lax.dot_general(left, right, (((0,), (0,)), ((), ())), preferred_element_type=F32)


def sigmoid(value):
    return 0.5 * jnp.tanh(0.5 * value) + 0.5


def row_mean(value):
    return jnp.mean(value, axis=-1, keepdims=True)


def norm_forward(mixed):
    centered = mixed - row_mean(mixed)
    inverse = lax.rsqrt(row_mean(centered * centered) + EPSILON)
    return centered * inverse, inverse


def norm_backward(normed, inverse, scaled):
    return inverse * (scaled - row_mean(scaled) - normed * row_mean(scaled * normed))


def one_hot(mask):
    return jnp.where(mask, 1.0, 0.0).astype(BF)


def as_columns(index):
    return jnp.transpose(index.astype(F32)).astype(jnp.int32)


def pick_matrix(columns, first, blocks, size):
    lanes = lax.broadcasted_iota(jnp.int32, (LANES, size), 1)
    parts = [one_hot(columns[:, b : b + 1] == lanes) for b in range(first, first + blocks)]
    return jnp.concatenate(parts, axis=0)


def place_matrix(rows, first, blocks, size):
    sublanes = lax.broadcasted_iota(jnp.int32, (size, LANES), 0)
    parts = [one_hot(rows[b : b + 1, :] == sublanes) for b in range(first, first + blocks)]
    return jnp.concatenate(parts, axis=1)


def call(kernel, outs, args, flops, scratch=()):
    moved = sum(a.size * a.dtype.itemsize for a in args)
    moved += sum(math.prod(s) * jnp.dtype(t).itemsize for s, t in outs)
    return pl.pallas_call(
        kernel,
        out_shape=[jax.ShapeDtypeStruct(s, t) for s, t in outs],
        in_specs=[pl.BlockSpec(memory_space=pltpu.SMEM if a.ndim == 1 else pltpu.VMEM) for a in args],
        out_specs=[pl.BlockSpec(memory_space=pltpu.VMEM)] * len(outs),
        scratch_shapes=list(scratch),
        compiler_params=pltpu.CompilerParams(vmem_limit_bytes=24 * 1024 * 1024),
        cost_estimate=pl.CostEstimate(flops=flops, bytes_accessed=moved, transcendentals=0),
    )(*args)


def halo_kernel(mesh_ref, index_ref, out_ref):
    columns = as_columns(index_ref[...])
    for c in range(3):
        out_ref[c] = dot(pick_matrix(columns, c, 1, mesh_ref.shape[0]), mesh_ref[...]).astype(BF)


def local_kernel(mesh_ref, grid_ref, w1, w3, w7, biases, dst_ref, part_ref, proj_ref):
    mesh = mesh_ref[...]
    dst_ref[...] = (dot(mesh, w1[...]) + biases[0:1, :]).astype(BF)
    part_ref[...] = dot(mesh, w3[...]) + biases[1:2, :]
    proj_ref[...] = (dot(grid_ref[...], w7[...]) + biases[2:3, :]).astype(BF)


def edge_forward_kernel(*refs):
    n_band = (len(refs) - 25) // 3
    tables, refs = refs[: 3 * n_band], refs[3 * n_band :]
    (dst_ref, source_ref, target_ref, w0, w2, w4, w5, w6, mesh_ref, part_ref, gains, send_ref) = refs[:12]
    (
        hidden_ref, slope_ref, normed_ref, inverse_ref, summed_ref, aggregate_ref, node_hidden_ref,
        node_slope_ref, node_normed_ref, node_inverse_ref, new_mesh_ref, outbound_ref,
    ) = refs[12:24]
    table_ref = refs[24]
    features = dst_ref.shape[1]
    mesh_rows = dst_ref.shape[0]
    for c in range(3):
        for j in range(n_band):
            table_ref[c, j * LANES : (j + 1) * LANES, :] = dot(tables[n_band * c + j][...], w0[...]).astype(BF)
    summed_ref[...] = jnp.zeros_like(summed_ref)

    def group(c, carry):
        source_columns = as_columns(source_ref[c])
        target_columns = as_columns(target_ref[c])
        targets = target_ref[c]
        table = table_ref[c]
        for half in range(2):
            preact = dot(pick_matrix(source_columns, 4 * half, 4, n_band * LANES), table)
            preact += dot(pick_matrix(target_columns, 4 * half, 4, mesh_rows), dst_ref[...])
            gate = sigmoid(preact)
            hidden = (preact * gate).astype(BF)
            normed, inverse = norm_forward(dot(hidden, w2[...]))
            normed = normed.astype(BF)
            rows = pl.ds(pl.multiple_of(c * 8 * LANES + half * 4 * LANES, 4 * LANES), 4 * LANES)
            hidden_ref[rows, :] = hidden
            slope_ref[rows, :] = (gate * (1.0 + preact * (1.0 - gate))).astype(BF)
            normed_ref[rows, :] = normed
            inverse_ref[rows, :] = inverse
            summed_ref[...] += dot(place_matrix(targets, 4 * half, 4, mesh_rows), normed)
        return carry

    lax.fori_loop(0, 3, group, 0)
    aggregate = (summed_ref[...] * gains[0:1, :]).astype(BF)
    aggregate_ref[...] = aggregate
    node_pre = part_ref[...] + dot(aggregate, w4[...])
    gate = sigmoid(node_pre)
    node_hidden = (node_pre * gate).astype(BF)
    node_hidden_ref[...] = node_hidden
    node_slope_ref[...] = gate * (1.0 + node_pre * (1.0 - gate))
    normed, inverse = norm_forward(dot(node_hidden, w5[...]))
    node_normed_ref[...] = normed
    node_inverse_ref[...] = inverse
    new_mesh = (mesh_ref[...].astype(F32) + normed * gains[1:2, :]).astype(BF)
    new_mesh_ref[...] = new_mesh
    value = dot(new_mesh, w6[...]).astype(BF)
    columns = as_columns(send_ref[...])
    for half in range(2):
        outbound_ref[half * 4 * LANES : (half + 1) * 4 * LANES, :] = dot(
            pick_matrix(columns, 4 * half, 4, mesh_rows), value
        ).astype(BF)


def decoder_kernel(
    received_ref, proj_ref, cot_ref, source_ref, w8, gains,
    slot_ref, proj_grad_ref, weight_ref, gain_ref, slot_sum, proj_sum,
):
    slots = received_ref.shape[0]
    columns = as_columns(source_ref[...])
    sources = source_ref[...]
    cot = cot_ref[...].astype(F32)
    scaled = cot * gains[2:3, :]
    scaled_mean = row_mean(scaled)
    for c in range(3):
        preact = dot(pick_matrix(columns, 4 * c, 4, slots), received_ref[...]) + proj_ref[...].astype(F32)
        gate = sigmoid(preact)
        hidden = (preact * gate).astype(BF)
        slope = gate * (1.0 + preact * (1.0 - gate))
        normed, inverse = norm_forward(dot(hidden, w8[...]))
        grad_mixed = (inverse * (scaled - scaled_mean - normed * row_mean(scaled * normed))).astype(BF)
        gain = jnp.sum(cot * normed, axis=0, keepdims=True)
        weight = t_dot(hidden, grad_mixed)
        grad_pre = (dot_t(grad_mixed, w8[...]) * slope).astype(BF)
        placed = dot(place_matrix(sources, 4 * c, 4, slots), grad_pre)
        if c == 0:
            gain_ref[...] = gain
            weight_ref[...] = weight
            slot_sum[...] = placed
            proj_sum[...] = grad_pre.astype(F32)
        else:
            gain_ref[...] += gain
            weight_ref[...] += weight
            slot_sum[...] += placed
            proj_sum[...] += grad_pre.astype(F32)
    slot_ref[...] = slot_sum[...].astype(BF)
    proj_grad_ref[...] = proj_sum[...].astype(BF)


def put_pieces(out_ref, slot, value):
    rounded = value.astype(BF)
    groups = value.shape[0] // TILE
    for h in range(2):
        block = rounded[:, h * LANES : (h + 1) * LANES].reshape(groups, TILE, LANES)
        out_ref[h * groups : (h + 1) * groups, :, slot * LANES : (slot + 1) * LANES] = block


def split_columns(core_ref, size):
    half = size // 2
    mine = core_ref[0] * half
    return pl.ds(pl.multiple_of(mine, half), half), pl.ds(pl.multiple_of(half - mine, half), half)


def put_outer(factor, core_ref, left_ref, right_ref, keep_ref, send_ref, slot):
    left = left_ref[...]
    for columns, out_ref in zip(split_columns(core_ref, right_ref.shape[1]), (keep_ref, send_ref)):
        put_pieces(out_ref, slot, t_dot(left, right_ref[:, columns]) * factor)


def put_whole(factor, core_ref, value_ref, keep_ref, send_ref, slot):
    for columns, out_ref in zip(split_columns(core_ref, value_ref.shape[1]), (keep_ref, send_ref)):
        put_pieces(out_ref, slot, value_ref[:, columns] * factor)


def grid_kernel(
    factor, core_ref, proj_grad_ref, cot_ref, grid_ref, w7, dec_weight, grad_ref, keep_ref, send_ref, bias_ref
):
    proj_grad = proj_grad_ref[...]
    grad_ref[...] = (cot_ref[...].astype(F32) + dot_t(proj_grad, w7[...])).astype(BF)
    put_outer(factor, core_ref, grid_ref, proj_grad_ref, keep_ref, send_ref, 0)
    put_whole(factor, core_ref, dec_weight, keep_ref, send_ref, 1)
    bias_ref[...] = jnp.sum(proj_grad.astype(F32), axis=0, keepdims=True)


def node_backward_kernel(
    returned_ref, send_ref, w6, w5, w4, node_normed_ref, node_inverse_ref, node_slope_ref, summed_ref, gains,
    value_grad_ref, new_grad_ref, out_grad_ref, pre_grad_ref, scaled_ref, gain_ref,
):
    mesh_rows = node_normed_ref.shape[0]
    value_grad = dot(place_matrix(send_ref[...], 0, 8, mesh_rows), returned_ref[...]).astype(BF)
    value_grad_ref[...] = value_grad
    new_grad = dot_t(value_grad, w6[...])
    new_grad_ref[...] = new_grad
    normed = node_normed_ref[...]
    out_grad = norm_backward(normed, node_inverse_ref[...], new_grad * gains[1:2, :]).astype(BF)
    out_grad_ref[...] = out_grad
    pre_grad = (dot_t(out_grad, w5[...]) * node_slope_ref[...]).astype(BF)
    pre_grad_ref[...] = pre_grad
    aggregate_grad = dot_t(pre_grad, w4[...])
    scaled_ref[...] = (aggregate_grad * gains[0:1, :]).astype(BF)
    gain_ref[0:1, :] = jnp.sum(aggregate_grad * summed_ref[...], axis=0, keepdims=True)
    gain_ref[1:2, :] = jnp.sum(new_grad * normed, axis=0, keepdims=True)


def node_weights_kernel(
    factor, core_ref, mesh_ref, aggregate_ref, node_hidden_ref, new_mesh_ref, pre_grad_ref, out_grad_ref,
    value_grad_ref, keep_ref, send_ref,
):
    put_outer(factor, core_ref, mesh_ref, pre_grad_ref, keep_ref, send_ref, 0)
    put_outer(factor, core_ref, aggregate_ref, pre_grad_ref, keep_ref, send_ref, 1)
    put_outer(factor, core_ref, node_hidden_ref, out_grad_ref, keep_ref, send_ref, 2)
    put_outer(factor, core_ref, new_mesh_ref, value_grad_ref, keep_ref, send_ref, 3)


def pair_kernel(*refs):
    out_ref = refs[-1]
    first = 0
    for keep_ref, got_ref in zip(refs[:-1:2], refs[1:-1:2]):
        width = keep_ref.shape[2]
        total = keep_ref[...].astype(F32) + got_ref[...].astype(F32)
        out_ref[:, :, first : first + width] = total.astype(BF)
        first += width


def share_kernel(chips, early_ref, late_ref, out_ref):
    own = PIECES // chips
    first = 0
    for ref in (early_ref, late_ref):
        width = ref.shape[2]
        total = ref[0:own].astype(F32)
        for k in range(1, chips):
            total += ref[k * own : (k + 1) * own].astype(F32)
        rounded = total.astype(BF)
        for copy in range(out_ref.shape[0]):
            out_ref[copy, :, :, first : first + width] = rounded
        first += width


def spread_kernel(order, place_ref, *refs):
    blocks, out_ref, small_ref = refs[:-2], refs[-2], refs[-1]
    step = pl.program_id(0)
    slot = jnp.int32(0)
    for k, which in enumerate(order):
        slot = jnp.where(step == k, which, slot)
    lanes = pl.ds(pl.multiple_of(slot * LANES, LANES), LANES)
    groups = out_ref.shape[1] // TILE
    for index, block_ref in enumerate(blocks):
        count = block_ref.shape[0]
        piece = place_ref[2 * index]
        rows = pl.ds(pl.multiple_of((piece % groups) * TILE, TILE), count * TILE)
        columns = pl.ds(pl.multiple_of((place_ref[2 * index + 1] * 2 + piece // groups) * LANES, LANES), LANES)
        out_ref[0, rows, columns] = block_ref[:, :, lanes].reshape(count * TILE, LANES).astype(F32)

        @pl.when((step == 0) & (piece % groups == 0))
        def _():
            small_ref[:, columns] = block_ref[0, :, len(order) * LANES :].astype(F32)


def edge_backward_kernel(
    scaled_ref, source_ref, target_ref, w2, hidden_ref, slope_ref, normed_ref, inverse_ref,
    table_ref, dst_ref, weight_ref, table_sum, dst_sum,
):
    mesh_rows = scaled_ref.shape[0]
    dst_sum[...] = jnp.zeros_like(dst_sum)
    weight_ref[...] = jnp.zeros_like(weight_ref)

    def group(c, carry):
        target_columns = as_columns(target_ref[c])
        targets = target_ref[c]
        sources = source_ref[c]
        for half in range(2):
            rows = pl.ds(pl.multiple_of(c * 8 * LANES + half * 4 * LANES, 4 * LANES), 4 * LANES)
            scaled = dot(pick_matrix(target_columns, 4 * half, 4, mesh_rows), scaled_ref[...])
            grad_mixed = norm_backward(normed_ref[rows, :].astype(F32), inverse_ref[rows, :], scaled).astype(BF)
            weight_ref[...] += t_dot(hidden_ref[rows, :], grad_mixed)
            grad_pre = (dot_t(grad_mixed, w2[...]) * slope_ref[rows, :].astype(F32)).astype(BF)
            dst_sum[...] += dot(place_matrix(targets, 4 * half, 4, mesh_rows), grad_pre)
            placed = dot(place_matrix(sources, 4 * half, 4, table_sum.shape[0]), grad_pre)
            if half == 0:
                table_sum[...] = placed
            else:
                table_ref[c] = (table_sum[...] + placed).astype(BF)
        return carry

    lax.fori_loop(0, 3, group, 0)
    dst_ref[...] = dst_sum[...].astype(BF)


def edge_weights_kernel(factor, core_ref, *refs):
    n_band = (len(refs) - 16) // 3
    tables = refs[: 3 * n_band]
    (
        table_grad_ref, mesh_ref, dst_grad_ref, edge_weight, new_grad_ref, pre_grad_ref, w1, w3,
        gains_ref, dec_gain_ref, grid_bias_ref, partial_ref, keep_ref, send_ref, source_sum, small_sum,
    ) = refs[3 * n_band :]
    total = None
    for c in range(3):
        for j in range(n_band):
            part = t_dot(tables[n_band * c + j][...], table_grad_ref[c, j * LANES : (j + 1) * LANES, :])
            total = part if total is None else total + part
    source_sum[...] = total
    put_whole(factor, core_ref, source_sum, keep_ref, send_ref, 0)
    put_outer(factor, core_ref, mesh_ref, dst_grad_ref, keep_ref, send_ref, 1)
    put_whole(factor, core_ref, edge_weight, keep_ref, send_ref, 2)
    dst_grad = dst_grad_ref[...]
    pre_grad = pre_grad_ref[...]
    small_sum[...] = jnp.zeros_like(small_sum)
    small_sum[0:1, :] = jnp.sum(dst_grad.astype(F32), axis=0, keepdims=True)
    small_sum[1:2, :] = jnp.sum(pre_grad.astype(F32), axis=0, keepdims=True)
    small_sum[2:3, :] = grid_bias_ref[...]
    small_sum[3:5, :] = gains_ref[...]
    small_sum[5:6, :] = dec_gain_ref[...]
    put_whole(factor, core_ref, small_sum, keep_ref, send_ref, 3)
    partial_ref[...] = new_grad_ref[...] + dot_t(pre_grad, w3[...]) + dot_t(dst_grad, w1[...])


def final_kernel(*refs):
    n_band = (len(refs) - 4) // 3
    parts = refs[: 3 * n_band]
    index_ref, partial_ref, w0, grad_ref = refs[3 * n_band :]
    mesh_rows = partial_ref.shape[0]
    src_grad = None
    for c in range(3):
        halo = parts[n_band * c][...].astype(F32)
        for j in range(1, n_band):
            halo += parts[n_band * c + j][...].astype(F32)
        part = dot(place_matrix(index_ref[...], c, 1, mesh_rows), halo.astype(BF))
        src_grad = part if src_grad is None else src_grad + part
    grad_ref[...] = (partial_ref[...] + dot_t(src_grad.astype(BF), w0[...])).astype(BF)


def routes(n_mesh, n_band):
    found = {}
    for c in range(3):
        for step in range(n_band):
            if c == 1 and step == 0:
                continue
            found[c, step] = [
                (((i - c + 1) % n_mesh) * n_band + (j + step) % n_band, i * n_band + j)
                for i in range(n_mesh)
                for j in range(n_band)
            ]
    return found


def swap(value):
    return lax.ppermute(value, "core", [(0, 1), (1, 0)])


def pad_rows(index, rows):
    return jnp.pad(index, ((0, rows - index.shape[0]), (0, 0)))


def body(
    mesh_latent, grid_latent, weights, biases, gains, cotangent, halo_index, edge_source, edge_target,
    block_count, decoder_send, decoder_source,
):
    n_band = lax.axis_size("z")
    n_mesh = lax.axis_size(("x", "y", "core"))
    mesh_rows, features = mesh_latent.shape
    grid_rows = grid_latent.shape[0]
    shards, slots_each = decoder_send.shape[1:]
    slots = shards * slots_each
    blocks, block = edge_source.shape[2:]
    edges = 3 * blocks * block
    square = 2 * features * features
    factor = 1.0 / math.sqrt(grid_rows * n_mesh * n_band)
    w = [weights[k] for k in range(9)]
    paths = routes(n_mesh, n_band)

    halo_rows = pad_rows(halo_index[0], 8)
    (outgoing,) = call(halo_kernel, [((3, LANES, features), BF)], [mesh_latent, halo_rows], 384 * square)
    tables = []
    for c in range(3):
        for step in range(n_band):
            tables.append(lax.ppermute(outgoing[c], AXES, paths[c, step]) if (c, step) in paths else outgoing[c])

    band = lax.axis_index("z")
    sources = (edge_source[0] - band * LANES) & (n_band * LANES - 1)
    live = jnp.arange(blocks, dtype=jnp.int32)[None, :, None] < block_count[0][:, None, None]
    targets = jnp.where(live, edge_target[0], -1)
    send_rows = decoder_send[0].reshape(slots // LANES, LANES)
    source_rows = pad_rows(decoder_source.reshape(3 * grid_rows // LANES, LANES), 16)

    dst_proj, node_part, grid_proj = call(
        local_kernel,
        [((mesh_rows, features), BF), ((mesh_rows, features), F32), ((grid_rows, features), BF)],
        [mesh_latent, grid_latent, w[1], w[3], w[7], biases],
        3 * mesh_rows * square,
    )
    wide, wide32 = ((mesh_rows, features), BF), ((mesh_rows, features), F32)
    (
        hidden, slope, normed, inverse, summed, aggregate, node_hidden, node_slope, node_normed, node_inverse,
        new_mesh, outbound,
    ) = call(
        edge_forward_kernel,
        [
            ((edges, features), BF), ((edges, features), BF), ((edges, features), BF), ((edges, 1), F32),
            wide32, wide, wide, wide32, wide32, ((mesh_rows, 1), F32), wide, ((slots, features), BF),
        ],
        tables + [dst_proj, sources, targets, w[0], w[2], w[4], w[5], w[6], mesh_latent, node_part, gains, send_rows],
        5 * edges * square,
        [pltpu.VMEM((3, n_band * LANES, features), BF)],
    )
    received = lax.all_to_all(
        outbound.reshape(shards, slots_each, features), AXES, split_axis=0, concat_axis=0, tiled=True
    ).reshape(slots, features)
    slot_grad, proj_grad, dec_weight, dec_gain = call(
        decoder_kernel,
        [((slots, features), BF), ((grid_rows, features), BF), ((features, features), F32), ((1, features), F32)],
        [received, grid_proj, cotangent, source_rows, w[8], gains],
        7 * 3 * grid_rows * square,
        [pltpu.VMEM((slots, features), F32), pltpu.VMEM((grid_rows, features), F32)],
    )
    returned = lax.all_to_all(
        slot_grad.reshape(shards, slots_each, features), AXES, split_axis=0, concat_axis=0, tiled=True
    ).reshape(slots, features)
    core = lax.axis_index("core")
    core_row = core[None]
    half = lambda count: [((PIECES, TILE, count * LANES), BF)] * 2
    grad_grid, late_keep, late_send, grid_bias = call(
        functools.partial(grid_kernel, factor),
        [((grid_rows, features), BF)] + half(2) + [((1, features), F32)],
        [core_row, proj_grad, cotangent, grid_latent, w[7], dec_weight],
        2 * grid_rows * square,
    )

    value_grad, new_grad, out_grad, pre_grad, scaled, node_gains = call(
        node_backward_kernel,
        [wide, wide32, wide, wide, wide, ((2, features), F32)],
        [returned, send_rows, w[6], w[5], w[4], node_normed, node_inverse, node_slope, summed, gains],
        5 * mesh_rows * square,
    )
    node_keep, node_send = call(
        functools.partial(node_weights_kernel, factor),
        half(4),
        [core_row, mesh_latent, aggregate, node_hidden, new_mesh, pre_grad, out_grad, value_grad],
        4 * mesh_rows * square,
    )
    (early,) = call(
        pair_kernel, [((PIECES, TILE, 6 * LANES), BF)], [late_keep, swap(late_send), node_keep, swap(node_send)], 0
    )
    early = lax.all_to_all(early, CHIPS, split_axis=0, concat_axis=0, tiled=True)
    table_grad, dst_grad, edge_weight = call(
        edge_backward_kernel,
        [((3, n_band * LANES, features), BF), wide, ((features, features), F32)],
        [scaled, sources, targets, w[2], hidden, slope, normed, inverse],
        5 * edges * square,
        [pltpu.VMEM((n_band * LANES, features), F32), pltpu.VMEM((mesh_rows, features), F32)],
    )
    parts = []
    for c in range(3):
        for step in range(n_band):
            sent = table_grad[c, step * LANES : (step + 1) * LANES]
            if (c, step) in paths:
                sent = lax.ppermute(sent, AXES, [(b, a) for a, b in paths[c, step]])
            parts.append(sent)
    partial, edge_keep, edge_send = call(
        functools.partial(edge_weights_kernel, factor),
        [wide32] + half(4),
        [core_row] + tables
        + [table_grad, mesh_latent, dst_grad, edge_weight, new_grad, pre_grad, w[1], w[3], node_gains, dec_gain, grid_bias],
        6 * mesh_rows * square,
        [pltpu.VMEM((features, features), F32), pltpu.VMEM((features, features), F32)],
    )
    (late,) = call(pair_kernel, [((PIECES, TILE, 4 * LANES), BF)], [edge_keep, swap(edge_send)], 0)
    late = lax.all_to_all(late, CHIPS, split_axis=0, concat_axis=0, tiled=True)
    (grad_mesh,) = call(
        final_kernel, [wide], parts + [halo_rows, partial, w[0]], 2 * mesh_rows * square
    )
    n_x, plane = lax.axis_size("x"), lax.axis_size(("y", "z"))
    own = PIECES // (n_x * plane)
    (shared,) = call(
        functools.partial(share_kernel, n_x * plane), [((plane, own, TILE, 10 * LANES), BF)], [early, late], 0
    )
    shared = lax.all_to_all(shared, ("y", "z"), split_axis=0, concat_axis=0, tiled=True)
    shared = shared.reshape(plane * own, TILE, 10 * LANES)
    blocks, places = [], []
    for step in range(n_x):
        block = lax.ppermute(shared, "x", [((i + step) % n_x, i) for i in range(n_x)]) if step else shared
        piece = (lax.axis_index("x") + step) % n_x * plane * own
        blocks += [block, swap(block)]
        places += [piece, core, piece, 1 - core]
    order = (6, 7, 8, 2, 3, 4, 5, 0, 1)
    whole = pl.BlockSpec(memory_space=pltpu.VMEM)
    grad_weights, small = pl.pallas_call(
        functools.partial(spread_kernel, order),
        grid=(9,),
        out_shape=[
            jax.ShapeDtypeStruct((9, features, features), F32), jax.ShapeDtypeStruct((TILE, features), F32)
        ],
        in_specs=[pl.BlockSpec(memory_space=pltpu.SMEM)] + [whole] * len(blocks),
        out_specs=[pl.BlockSpec((1, features, features), lambda k: (k, 0, 0)), whole],
        compiler_params=pltpu.CompilerParams(vmem_limit_bytes=24 * 1024 * 1024),
        cost_estimate=pl.CostEstimate(flops=0, bytes_accessed=14_000_000, transcendentals=0),
    )(jnp.stack(places).astype(jnp.int32), *blocks)
    return grad_mesh, grad_grid, grad_weights, small[0:3], small[3:6]


def solution(mesh):
    n_mesh, n_band = mesh.devices.shape
    side = math.isqrt(n_mesh // 2)
    axes = jax.sharding.Mesh(mesh.devices.reshape(n_mesh // (2 * side), side, 2, n_band), AXES)
    both = P(AXES)
    return jax.shard_map(
        body,
        mesh=axes,
        in_specs=(both, both, P(), P(), P(), both, both, both, both, both, both, P(None, AXES)),
        out_specs=(both, both, P(), P(), P()),
        check_vma=False,
    )
```

```python
import functools
import math

import jax
import jax.numpy as jnp
from jax import lax
from jax.experimental import pallas as pl
from jax.experimental.pallas import tpu as pltpu
from jax.sharding import PartitionSpec as P

EPSILON = 1e-05
BF = jnp.bfloat16
F32 = jnp.float32
LANES = 128
TILE = 16
PIECES = 64
AXES = ("x", "y", "core", "z")
CHIPS = ("x", "y", "z")


def dot(left, right):
    return jnp.dot(left, right, preferred_element_type=F32)


def dot_t(left, right):
    return lax.dot_general(left, right, (((1,), (1,)), ((), ())), preferred_element_type=F32)


def t_dot(left, right):
    return lax.dot_general(left, right, (((0,), (0,)), ((), ())), preferred_element_type=F32)


def sigmoid(value):
    return 0.5 * jnp.tanh(0.5 * value) + 0.5


def row_mean(value):
    return jnp.mean(value, axis=-1, keepdims=True)


def norm_forward(mixed):
    centered = mixed - row_mean(mixed)
    inverse = lax.rsqrt(row_mean(centered * centered) + EPSILON)
    return centered * inverse, inverse


def norm_backward(normed, inverse, scaled):
    return inverse * (scaled - row_mean(scaled) - normed * row_mean(scaled * normed))


def one_hot(mask):
    return jnp.where(mask, 1.0, 0.0).astype(BF)


def as_columns(index):
    return jnp.transpose(index.astype(F32)).astype(jnp.int32)


def pick_matrix(columns, first, blocks, size):
    lanes = lax.broadcasted_iota(jnp.int32, (LANES, size), 1)
    parts = [one_hot(columns[:, b : b + 1] == lanes) for b in range(first, first + blocks)]
    return jnp.concatenate(parts, axis=0)


def place_matrix(rows, first, blocks, size):
    sublanes = lax.broadcasted_iota(jnp.int32, (size, LANES), 0)
    parts = [one_hot(rows[b : b + 1, :] == sublanes) for b in range(first, first + blocks)]
    return jnp.concatenate(parts, axis=1)


class Operand:
    def __init__(self, source, buffer, semaphore):
        self.source, self.buffer, self.semaphore = source, buffer, semaphore
        self.shape, self.dtype = buffer.shape, buffer.dtype
        self.arrived = False

    def copies(self):
        if not isinstance(self.source, list):
            return [pltpu.make_async_copy(self.source, self.buffer, self.semaphore.at[0])]
        size = self.shape[0] // len(self.source)
        return [
            pltpu.make_async_copy(source, self.buffer.at[pl.ds(k * size, size)], self.semaphore.at[k])
            for k, source in enumerate(self.source)
        ]

    def start(self):
        for copy in self.copies():
            copy.start()

    def get(self):
        if not self.arrived:
            for copy in self.copies():
                copy.wait()
            self.arrived = True
        return self.buffer

    def __getitem__(self, index):
        return self.get()[index]


class Stream(Operand):
    def run(self, number):
        count = self.semaphore.shape[0]
        size = self.shape[0] // count
        rows = pl.ds(number * size if isinstance(number, int) else pl.multiple_of(number * size, size), size)
        return pltpu.make_async_copy(self.source.at[rows], self.buffer.at[rows], self.semaphore.at[number])

    def arrive(self, number):
        self.run(number).wait()

    def get(self):
        return self.buffer


class Result:
    def __init__(self, target, buffer, semaphore):
        self.target, self.buffer, self.semaphore = target, buffer, semaphore
        self.shape, self.dtype = buffer.shape, buffer.dtype
        self.sent = False

    def __getitem__(self, index):
        return self.buffer[index]

    def __setitem__(self, index, value):
        self.buffer[index] = value

    def send(self, rows=None):
        self.sent = True
        if rows is None:
            pltpu.make_async_copy(self.buffer, self.target, self.semaphore).start()
        else:
            pltpu.make_async_copy(self.buffer.at[rows], self.target.at[rows], self.semaphore).start()

    def finish(self):
        if not self.sent:
            self.send()
        pltpu.make_async_copy(self.buffer, self.target, self.semaphore).wait()


def call(kernel, outs, args, flops, scratch=(), streams=(), runs=1, after=()):
    arrays, places, shapes, kinds = [], [], [], []

    def place(array):
        for k, other in enumerate(arrays):
            if other is array:
                return k
        arrays.append(array)
        return len(arrays) - 1

    for arg in args:
        if isinstance(arg, list):
            places.append([place(array) for array in arg])
            shapes.append((len(arg) * arg[0].shape[0],) + arg[0].shape[1:])
            kinds.append(arg[0].dtype)
            continue
        array, entry = arg if isinstance(arg, tuple) else (arg, None)
        places.append((place(array), entry))
        shapes.append(array.shape if entry is None else array.shape[1:])
        kinds.append(array.dtype)
    scalar = [len(shape) == 1 for shape in shapes]
    buffers, semaphores = [], []
    for number, where in enumerate(places):
        if not scalar[number]:
            buffers.append(pltpu.VMEM(shapes[number], kinds[number]))
            count = len(where) if isinstance(where, list) else runs if number in streams else 1
            semaphores.append(pltpu.SemaphoreType.DMA((count,)))
    for array in after:
        place(array)
    out_shapes = [jax.ShapeDtypeStruct(shape, kind) for shape, kind in outs]
    out_buffers = [pltpu.VMEM(shape, kind) for shape, kind in outs]
    operands = arrays
    n_in, n_out, n_buf = len(operands), len(out_shapes), len(buffers)

    def wrapped(*refs):
        sources, targets = refs[:n_in], refs[n_in : n_in + n_out]
        rest = refs[n_in + n_out :]
        in_buffers, rest = rest[:n_buf], rest[n_buf:]
        out_refs, rest = rest[:n_out], rest[n_out:]
        in_semaphores, rest = rest[:n_buf], rest[n_buf:]
        out_semaphore, user = rest[0], rest[1:]
        inputs, position = [], 0
        for number, where in enumerate(places):
            if scalar[number]:
                inputs.append(sources[where[0]])
                continue
            if isinstance(where, list):
                source = [sources[k] for k in where]
            else:
                source = sources[where[0]] if where[1] is None else sources[where[0]].at[where[1]]
            kind = Stream if number in streams else Operand
            inputs.append(kind(source, in_buffers[position], in_semaphores[position]))
            position += 1
        for item in inputs:
            if isinstance(item, Operand) and not isinstance(item, Stream):
                item.start()
        for number in range(runs if streams else 0):
            for item in inputs:
                if isinstance(item, Stream):
                    item.run(number).start()
        results = []
        for number in range(n_out):
            results.append(Result(targets[number], out_refs[number], out_semaphore.at[number]))
        kernel(*inputs, *results, *user)
        for item in inputs:
            if isinstance(item, Operand) and not isinstance(item, Stream):
                item.get()
        for item in results:
            item.finish()

    moved = sum(math.prod(s) * t.itemsize for s, t in zip(shapes, kinds))
    moved += sum(math.prod(s) * jnp.dtype(t).itemsize for s, t in outs)
    return pl.pallas_call(
        wrapped,
        out_shape=out_shapes,
        in_specs=[pl.BlockSpec(memory_space=pltpu.SMEM if a.ndim == 1 else pl.ANY) for a in operands],
        out_specs=[pl.BlockSpec(memory_space=pl.ANY)] * n_out,
        scratch_shapes=buffers + out_buffers + semaphores + [pltpu.SemaphoreType.DMA((n_out,))] + list(scratch),
        compiler_params=pltpu.CompilerParams(vmem_limit_bytes=56 * 1024 * 1024),
        cost_estimate=pl.CostEstimate(flops=flops, bytes_accessed=moved, transcendentals=0),
    )(*operands)


def halo_kernel(mesh_ref, index_ref, *out_refs):
    columns = as_columns(index_ref[...])
    for c in (1, 0, 2):
        out_refs[c][...] = dot(pick_matrix(columns, c, 1, mesh_ref.shape[0]), mesh_ref[...]).astype(BF)
        out_refs[c].send()


def diagonal():
    shape = (LANES, LANES)
    return lax.broadcasted_iota(jnp.int32, shape, 0) == lax.broadcasted_iota(jnp.int32, shape, 1)


def column_as_rows(column):
    parts = [column[k : k + LANES] for k in range(0, column.shape[0], LANES)]
    return jnp.concatenate(
        [jnp.sum(jnp.where(diagonal(), part, 0.0), axis=0, keepdims=True) for part in parts], axis=0
    )


def rows_as_column(rows):
    parts = [rows[k : k + 1] for k in range(rows.shape[0])]
    return jnp.concatenate(
        [jnp.sum(jnp.where(diagonal(), part, 0.0), axis=1, keepdims=True) for part in parts], axis=0
    )


def live_rows(index, count):
    blocks = lax.broadcasted_iota(jnp.int32, index.shape, 0)
    return jnp.where(blocks < count, index, -1)


def edge_forward_kernel(
    n_band, count_ref, band_ref, mesh_ref, w1, tables, w0, source_ref, target_ref, biases, w2, w3, w4, w5, w6, gains,
    send_ref, hidden_ref, slope_ref, normed_ref, inverse_ref, aggregate_ref, node_hidden_ref, node_slope_ref,
    node_normed_ref, node_inverse_ref, new_mesh_ref, outbound_ref, table_ref, dst_ref, summed_ref,
):
    mesh_rows = mesh_ref.shape[0]
    size = n_band * LANES
    dst_ref[...] = (dot(mesh_ref[...], w1[...]) + biases[0:1, :]).astype(BF)
    table_ref[...] = dot(tables[...], w0[...]).astype(BF)
    summed_ref[...] = jnp.zeros(summed_ref.shape, F32)
    w2, source_ref, target_ref = w2.get(), source_ref.get(), target_ref.get()

    def group(c, carry):
        source_columns = as_columns((source_ref[c] - band_ref[0] * LANES) & (size - 1))
        targets = live_rows(target_ref[c], count_ref[c])
        target_columns = as_columns(targets)
        table = table_ref[pl.ds(pl.multiple_of(c * size, size), size), :]
        preact = dot(pick_matrix(source_columns, 0, 8, size), table)
        preact += dot(pick_matrix(target_columns, 0, 8, mesh_rows), dst_ref[...])
        gate = sigmoid(preact)
        hidden = (preact * gate).astype(BF)
        normed, inverse = norm_forward(dot(hidden, w2[...]))
        normed = normed.astype(BF)
        rows = pl.ds(pl.multiple_of(c * 8 * LANES, 8 * LANES), 8 * LANES)
        hidden_ref[rows, :] = hidden
        slope_ref[rows, :] = (gate * (1.0 + preact * (1.0 - gate))).astype(BF)
        normed_ref[rows, :] = normed
        inverse_ref[c] = column_as_rows(inverse)
        summed_ref[...] += dot(place_matrix(targets, 0, 8, mesh_rows), normed)
        for out_ref in (hidden_ref, slope_ref, normed_ref):
            out_ref.send(rows)
        return carry

    lax.fori_loop(0, 3, group, 0)
    for out_ref in (hidden_ref, slope_ref, normed_ref):
        out_ref.sent = True
    w3, w4, w5, w6, gains, send_ref = (item.get() for item in (w3, w4, w5, w6, gains, send_ref))
    aggregate = (summed_ref[...] * gains[0:1, :]).astype(BF)
    aggregate_ref[...] = aggregate
    node_pre = dot(mesh_ref[...], w3[...]) + biases[1:2, :] + dot(aggregate, w4[...])
    gate = sigmoid(node_pre)
    node_hidden = (node_pre * gate).astype(BF)
    node_hidden_ref[...] = node_hidden
    node_slope_ref[...] = (gate * (1.0 + node_pre * (1.0 - gate))).astype(BF)
    normed, inverse = norm_forward(dot(node_hidden, w5[...]))
    node_normed_ref[...] = normed.astype(BF)
    node_inverse_ref[...] = column_as_rows(inverse)
    new_mesh = (mesh_ref[...].astype(F32) + normed * gains[1:2, :]).astype(BF)
    new_mesh_ref[...] = new_mesh
    for out_ref in (aggregate_ref, node_hidden_ref, node_slope_ref, node_normed_ref, node_inverse_ref, new_mesh_ref):
        out_ref.send()
    value = dot(new_mesh, w6[...]).astype(BF)
    outbound_ref[...] = dot(pick_matrix(as_columns(send_ref[...]), 0, 8, mesh_rows), value).astype(BF)


def decoder_kernel(
    grid_ref, w7, biases, cot_ref, gains, source_ref, received_ref, w8,
    slot_ref, proj_grad_ref, weight_ref, gain_ref, slot_sum, proj_sum, proj_ref,
):
    slots = received_ref.shape[0]
    for item in (grid_ref, w7, biases, cot_ref, gains, source_ref, received_ref, w8):
        item.get()
    proj_ref[...] = (dot(grid_ref[...], w7[...]) + biases[2:3, :]).astype(BF).astype(F32)
    columns = as_columns(source_ref[...])
    sources = source_ref[...]
    cot = cot_ref[...].astype(F32)
    scaled = cot * gains[2:3, :]
    scaled_mean = row_mean(scaled)
    for c in range(3):
        preact = dot(pick_matrix(columns, 4 * c, 4, slots), received_ref[...]) + proj_ref[...]
        gate = sigmoid(preact)
        hidden = (preact * gate).astype(BF)
        slope = gate * (1.0 + preact * (1.0 - gate))
        normed, inverse = norm_forward(dot(hidden, w8[...]))
        grad_mixed = (inverse * (scaled - scaled_mean - normed * row_mean(scaled * normed))).astype(BF)
        gain = jnp.sum(cot * normed, axis=0, keepdims=True)
        weight = t_dot(hidden, grad_mixed)
        grad_pre = (dot_t(grad_mixed, w8[...]) * slope).astype(BF)
        placed = dot(place_matrix(sources, 4 * c, 4, slots), grad_pre)
        if c == 0:
            gain_ref[...] = gain
            weight_ref[...] = weight
            slot_sum[...] = placed
            proj_sum[...] = grad_pre.astype(F32)
        elif c == 1:
            gain_ref[...] += gain
            weight_ref[...] += weight
            slot_sum[...] += placed
            proj_sum[...] += grad_pre.astype(F32)
        else:
            slot_ref[...] = (slot_sum[...] + placed).astype(BF)
            gain_ref[...] += gain
            weight_ref[...] += weight
            proj_grad_ref[...] = (proj_sum[...] + grad_pre.astype(F32)).astype(BF)


def put_pieces(out_ref, slot, value):
    rounded = value.astype(BF)
    groups = value.shape[0] // TILE
    for h in range(2):
        block = rounded[:, h * LANES : (h + 1) * LANES].reshape(groups, TILE, LANES)
        out_ref[h * groups : (h + 1) * groups, :, slot * LANES : (slot + 1) * LANES] = block


def split_columns(core_ref, size):
    half = size // 2
    mine = core_ref[0] * half
    return pl.ds(pl.multiple_of(mine, half), half), pl.ds(pl.multiple_of(half - mine, half), half)


def put_whole(factor, core_ref, value_ref, keep_ref, send_ref, slot):
    for columns, out_ref in zip(split_columns(core_ref, value_ref.shape[1]), (keep_ref, send_ref)):
        put_pieces(out_ref, slot, value_ref[:, columns] * factor)


def put_outer(factor, core_ref, left_ref, right_ref, keep_ref, send_ref, slot, product_ref):
    product_ref[...] = t_dot(left_ref[...], right_ref[...])
    put_whole(factor, core_ref, product_ref, keep_ref, send_ref, slot)


def grid_kernel(
    factor, core_ref, proj_grad_ref, grid_ref, dec_weight, cot_ref, w7, keep_ref, send_ref, grad_ref, bias_ref,
    product_ref,
):
    put_outer(factor, core_ref, grid_ref, proj_grad_ref, keep_ref, send_ref, 0, product_ref)
    put_whole(factor, core_ref, dec_weight, keep_ref, send_ref, 1)
    keep_ref.send()
    send_ref.send()
    proj_grad = proj_grad_ref[...]
    grad_ref[...] = (cot_ref[...].astype(F32) + dot_t(proj_grad, w7[...])).astype(BF)
    grad_ref.send()
    bias_ref[...] = jnp.sum(proj_grad.astype(F32), axis=0, keepdims=True)


def node_backward_kernel(
    factor, core_ref, send_ref, returned_ref, w6, node_normed_ref, node_inverse_ref, gains, w5, node_slope_ref, w4,
    aggregate_ref, mesh_ref, node_hidden_ref, new_mesh_ref,
    new_grad_ref, pre_grad_ref, scaled_ref, gain_ref, out_keep, out_send, value_grad_ref, out_grad_ref,
    product_ref,
):
    mesh_rows = node_normed_ref.shape[0]
    value_grad = dot(place_matrix(send_ref[...], 0, 8, mesh_rows), returned_ref[...]).astype(BF)
    value_grad_ref[...] = value_grad
    new_grad = dot_t(value_grad, w6[...])
    new_grad_ref[...] = new_grad
    normed = node_normed_ref[...].astype(F32)
    inverse = rows_as_column(node_inverse_ref[...])
    out_grad = norm_backward(normed, inverse, new_grad * gains[1:2, :]).astype(BF)
    out_grad_ref[...] = out_grad
    pre_grad = (dot_t(out_grad, w5[...]) * node_slope_ref[...].astype(F32)).astype(BF)
    pre_grad_ref[...] = pre_grad
    aggregate_grad = dot_t(pre_grad, w4[...])
    scaled_ref[...] = (aggregate_grad * gains[0:1, :]).astype(BF)
    summed = aggregate_ref[...].astype(F32)
    gain_ref[0:1, :] = jnp.sum(aggregate_grad * summed, axis=0, keepdims=True) / gains[0:1, :]
    gain_ref[1:2, :] = jnp.sum(new_grad * normed, axis=0, keepdims=True)
    for item in (new_grad_ref, pre_grad_ref, scaled_ref):
        item.send()
    put_outer(factor, core_ref, mesh_ref, pre_grad_ref, out_keep, out_send, 0, product_ref)
    put_outer(factor, core_ref, aggregate_ref, pre_grad_ref, out_keep, out_send, 1, product_ref)
    put_outer(factor, core_ref, node_hidden_ref, out_grad_ref, out_keep, out_send, 2, product_ref)
    put_outer(factor, core_ref, new_mesh_ref, value_grad_ref, out_keep, out_send, 3, product_ref)


def pair_kernel(*refs):
    out_ref = refs[-1]
    first = 0
    for keep_ref, got_ref in zip(refs[:-1:2], refs[1:-1:2]):
        width = keep_ref.shape[2]
        total = keep_ref[...].astype(F32) + got_ref[...].astype(F32)
        out_ref[:, :, first : first + width] = total.astype(BF)
        first += width


def share_kernel(chips, *refs):
    out_ref = refs[-1]
    own = PIECES // chips
    first = 0
    for got_ref in refs[:-1]:
        got_ref = got_ref.get()
        width = got_ref.shape[2]
        total = got_ref[0:own].astype(F32)
        for k in range(1, chips):
            total += got_ref[k * own : (k + 1) * own].astype(F32)
        rounded = total.astype(BF)
        for copy in range(out_ref.shape[0]):
            out_ref[copy, :, :, first : first + width] = rounded
        first += width


def spread_kernel(slots, place_ref, *refs):
    blocks, (biases_ref, gains_ref, out_ref) = refs[:-3], refs[-3:]
    groups = out_ref.shape[1] // TILE
    blocks = [block_ref.get() for block_ref in blocks]
    where = []
    for index, block_ref in enumerate(blocks):
        count = block_ref.shape[0]
        piece = place_ref[2 * index]
        lanes = (place_ref[2 * index + 1] * 2 + piece // groups) * LANES
        rows = pl.ds(pl.multiple_of((piece % groups) * TILE, TILE), count * TILE)
        where.append((count, piece, rows, pl.ds(pl.multiple_of(lanes, LANES), LANES)))
    for (count, piece, _, columns), block_ref in zip(where, blocks):

        @pl.when(piece % groups == 0)
        def _():
            value = block_ref[0, :, len(slots) * LANES :].astype(F32)
            biases_ref[:, columns] = value[0:3]
            gains_ref[:, columns] = value[3:6]

    for entry, slot in enumerate(slots):
        for (count, _, rows, columns), block_ref in zip(where, blocks):
            value = block_ref[:, :, slot * LANES : (slot + 1) * LANES]
            out_ref[entry, rows, columns] = value.reshape(count * TILE, LANES).astype(F32)
        out_ref.send(pl.ds(entry, 1))


def edge_backward_kernel(
    factor, n_band, count_ref, core_ref, band_ref, source_ref, target_ref, scaled_ref, w2, inverse_ref, normed_ref,
    hidden_ref, slope_ref, mesh_ref, tables, pre_grad_ref, grid_bias_ref, gains_ref, dec_gain_ref,
    table_ref, dst_ref, keep_ref, send_ref, dst_sum, weight_sum, small_sum, right_ref,
):
    mesh_rows = scaled_ref.shape[0]
    size = n_band * LANES
    dst_sum[...] = jnp.zeros(dst_sum.shape, F32)
    weight_sum[...] = jnp.zeros(weight_sum.shape, F32)
    scaled_ref, w2, source_ref, target_ref, inverse_ref = (
        item.get() for item in (scaled_ref, w2, source_ref, target_ref, inverse_ref)
    )

    def group(c, carry):
        for item in (normed_ref, hidden_ref, slope_ref):
            item.arrive(c)
        targets = live_rows(target_ref[c], count_ref[c])
        rows = pl.ds(pl.multiple_of(c * 8 * LANES, 8 * LANES), 8 * LANES)
        scaled = dot(pick_matrix(as_columns(targets), 0, 8, mesh_rows), scaled_ref[...])
        inverse = rows_as_column(inverse_ref[c])
        grad_mixed = norm_backward(normed_ref[rows, :].astype(F32), inverse, scaled).astype(BF)
        weight_sum[...] += t_dot(hidden_ref[rows, :], grad_mixed)
        grad_pre = (dot_t(grad_mixed, w2[...]) * slope_ref[rows, :].astype(F32)).astype(BF)
        dst_sum[...] += dot(place_matrix(targets, 0, 8, mesh_rows), grad_pre)
        placed = dot(place_matrix(source_ref[c], 0, 8, size), grad_pre).astype(BF)
        for j in range(n_band):
            table_ref[j, c] = placed[j * LANES : (j + 1) * LANES, :]
            there = lax.rem(j + n_band - band_ref[0], n_band)
            right_ref[pl.ds(pl.multiple_of((c * n_band + there) * LANES, LANES), LANES), :] = placed[
                j * LANES : (j + 1) * LANES, :
            ]
        return carry

    lax.fori_loop(0, 3, group, 0)
    table_ref.send()
    dst_grad = dst_sum[...].astype(BF)
    dst_ref[...] = dst_grad
    dst_ref.send()
    put_whole(factor, core_ref, weight_sum, keep_ref, send_ref, 2)
    put_outer(factor, core_ref, tables, right_ref, keep_ref, send_ref, 0, small_sum)
    put_outer(factor, core_ref, mesh_ref, dst_ref, keep_ref, send_ref, 1, weight_sum)
    small_sum[...] = jnp.zeros(small_sum.shape, F32)
    small_sum[0:1, :] = jnp.sum(dst_grad.astype(F32), axis=0, keepdims=True)
    small_sum[1:2, :] = jnp.sum(pre_grad_ref[...].astype(F32), axis=0, keepdims=True)
    small_sum[2:3, :] = grid_bias_ref[...]
    small_sum[3:5, :] = gains_ref[...]
    small_sum[5:6, :] = dec_gain_ref[...]
    put_whole(factor, core_ref, small_sum, keep_ref, send_ref, 3)


def band_sum_kernel(*refs):
    blocks, outs = refs[:-3], refs[-3:]
    for c in (0, 2, 1):
        total = blocks[0][c].astype(F32)
        for block_ref in blocks[1:]:
            total += block_ref[c].astype(F32)
        outs[c][...] = total.astype(BF)
        outs[c].send()


def final_kernel(
    pre_grad_ref, w3, dst_grad_ref, w1, new_grad_ref, index_ref, next_ref, own_ref, prev_ref, w0, grad_ref
):
    mesh_rows = new_grad_ref.shape[0]
    partial = new_grad_ref[...] + dot_t(pre_grad_ref[...], w3[...]) + dot_t(dst_grad_ref[...], w1[...])
    halo = jnp.concatenate([next_ref[...], own_ref[...], prev_ref[...]], axis=0)
    src_grad = dot(place_matrix(index_ref[...], 0, 3, mesh_rows), halo)
    grad_ref[...] = (partial + dot_t(src_grad.astype(BF), w0[...])).astype(BF)


def routes(n_mesh, n_band):
    found = {}
    for c in range(3):
        for step in range(n_band):
            if c == 1 and step == 0:
                continue
            found[c, step] = [
                (((i - c + 1) % n_mesh) * n_band + (j + step) % n_band, i * n_band + j)
                for i in range(n_mesh)
                for j in range(n_band)
            ]
    return found


def swap(value):
    return lax.ppermute(value, "core", [(0, 1), (1, 0)])


def pad_rows(index, rows):
    return jnp.pad(index, ((0, rows - index.shape[0]), (0, 0)))


def body(
    mesh_latent, grid_latent, weights, biases, gains, cotangent, halo_index, edge_source, edge_target,
    block_count, decoder_send, decoder_source,
):
    n_band = lax.axis_size("z")
    n_mesh = lax.axis_size(("x", "y", "core"))
    n_x, plane = lax.axis_size("x"), lax.axis_size(("y", "z"))
    chips = n_x * plane
    own = PIECES // chips
    mesh_rows, features = mesh_latent.shape
    grid_rows = grid_latent.shape[0]
    shards, slots_each = decoder_send.shape[1:]
    slots = shards * slots_each
    edges = 3 * edge_source.shape[2] * edge_source.shape[3]
    square = 2 * features * features
    factor = 1.0 / math.sqrt(grid_rows * n_mesh * n_band)
    w = [(weights, k) for k in range(9)]
    paths = routes(n_mesh, n_band)
    core, band = lax.axis_index("core"), lax.axis_index("z")
    core_row, band_row = core[None], band[None]
    sources, targets, counts = edge_source[0], edge_target[0], block_count[0]
    wide, wide32 = ((mesh_rows, features), BF), ((mesh_rows, features), F32)
    block = ((LANES, features), BF)

    def half(count):
        return [((PIECES, TILE, count * LANES), BF)] * 2

    halo_rows = pad_rows(halo_index[0], 8)
    outgoing = call(halo_kernel, [block] * 3, [mesh_latent, halo_rows], 384 * square)
    tables = []
    for c in range(3):
        for step in range(n_band):
            tables.append(lax.ppermute(outgoing[c], AXES, paths[c, step]) if (c, step) in paths else outgoing[c])

    send_rows = decoder_send[0].reshape(slots // LANES, LANES)
    source_rows = pad_rows(decoder_source.reshape(3 * grid_rows // LANES, LANES), 16)
    small_inverse = ((mesh_rows // LANES, LANES), F32)
    (
        hidden, slope, normed, inverse, aggregate, node_hidden, node_slope, node_normed, node_inverse, new_mesh, outbound,
    ) = call(
        functools.partial(edge_forward_kernel, n_band),
        [
            ((edges, features), BF), ((edges, features), BF), ((edges, features), BF), (targets.shape, F32),
            wide, wide, wide, wide, small_inverse, wide, ((slots, features), BF),
        ],
        [counts, band_row, mesh_latent, w[1], tables]
        + [w[0], sources, targets, biases, w[2], w[3], w[4], w[5], w[6], gains, send_rows],
        5 * edges * square,
        [
            pltpu.VMEM((3 * n_band * LANES, features), BF), pltpu.VMEM((mesh_rows, features), BF),
            pltpu.VMEM((mesh_rows, features), F32),
        ],
    )
    received = lax.all_to_all(
        outbound.reshape(shards, slots_each, features), AXES, split_axis=0, concat_axis=0, tiled=True
    ).reshape(slots, features)
    slot_grad, proj_grad, dec_weight, dec_gain = call(
        decoder_kernel,
        [((slots, features), BF), ((grid_rows, features), BF), ((features, features), F32), ((1, features), F32)],
        [grid_latent, w[7], biases, cotangent, gains, source_rows, received, w[8]],
        7 * 3 * grid_rows * square,
        [
            pltpu.VMEM((slots, features), F32), pltpu.VMEM((grid_rows, features), F32),
            pltpu.VMEM((grid_rows, features), F32),
        ],
    )
    returned = lax.all_to_all(
        slot_grad.reshape(shards, slots_each, features), AXES, split_axis=0, concat_axis=0, tiled=True
    ).reshape(slots, features)
    late_keep, late_send, grad_grid, grid_bias = call(
        functools.partial(grid_kernel, factor),
        half(2) + [((grid_rows, features), BF), ((1, features), F32)],
        [core_row, proj_grad, grid_latent, dec_weight, cotangent, w[7]],
        2 * grid_rows * square,
        [pltpu.VMEM((features, features), F32)],
    )
    late_got = swap(late_send)
    returned, late_keep, late_got = lax.optimization_barrier((returned, late_keep, late_got))
    new_grad, pre_grad, scaled, node_gains, node_keep, node_send = call(
        functools.partial(node_backward_kernel, factor),
        [wide32, wide, wide, ((2, features), F32)] + half(4),
        [
            core_row, send_rows, returned, w[6], node_normed, node_inverse, gains, w[5], node_slope, w[4],
            aggregate, mesh_latent, node_hidden, new_mesh,
        ],
        9 * mesh_rows * square,
        [
            pltpu.VMEM((mesh_rows, features), BF), pltpu.VMEM((mesh_rows, features), BF),
            pltpu.VMEM((features, features), F32),
        ],
    )
    (early,) = call(
        pair_kernel, [((PIECES, TILE, 6 * LANES), BF)], [late_keep, late_got, node_keep, swap(node_send)], 0
    )
    early = lax.all_to_all(early, CHIPS, split_axis=0, concat_axis=0, tiled=True)
    square_shape = (features, features)
    table_grad, dst_grad, edge_keep, edge_send = call(
        functools.partial(edge_backward_kernel, factor, n_band),
        [((n_band, 3, LANES, features), BF), wide] + half(4),
        [
            counts, core_row, band_row, sources, targets, scaled, w[2], inverse, normed, hidden, slope, mesh_latent,
            tables, pre_grad, grid_bias, node_gains, dec_gain,
        ],
        7 * edges * square,
        [
            pltpu.VMEM((mesh_rows, features), F32), pltpu.VMEM(square_shape, F32), pltpu.VMEM(square_shape, F32),
            pltpu.VMEM((3 * n_band * LANES, features), BF),
        ],
        streams=(8, 9, 10),
        runs=3,
    )
    edge_got = swap(edge_send)
    (late,) = call(
        pair_kernel, [((PIECES, TILE, 4 * LANES), BF)], [edge_keep, edge_got], 0, after=[early]
    )
    late = lax.all_to_all(late, CHIPS, split_axis=0, concat_axis=0, tiled=True)
    (shared,) = call(
        functools.partial(share_kernel, chips), [((plane, own, TILE, 10 * LANES), BF)], [early, late], 0
    )
    block_rows = lax.all_to_all(shared, ("y", "z"), split_axis=0, concat_axis=0, tiled=True)
    block_rows = block_rows.reshape(plane * own, TILE, 10 * LANES)
    table_grad, _ = lax.optimization_barrier((table_grad, shared))
    swept = []
    for step in range(n_band):
        piece = lax.dynamic_index_in_dim(table_grad, lax.rem(band + step, n_band), 0, keepdims=False)
        swept.append(
            lax.ppermute(piece, "z", [(i, (i + step) % n_band) for i in range(n_band)]) if step else piece
        )
    blocks, places = [], []
    for step in range(n_x):
        moved = block_rows
        if step:
            moved = lax.ppermute(moved, "x", [((i + step) % n_x, i) for i in range(n_x)])
        piece = (lax.axis_index("x") + step) % n_x * plane * own
        blocks += [moved, swap(moved)]
        places += [piece, core, piece, 1 - core]
    summed_next, summed_own, summed_prev = call(band_sum_kernel, [block] * 3, swept, 0, after=[block_rows])
    row = ("x", "y", "core")
    summed_next = lax.ppermute(summed_next, row, [(i, (i + 1) % n_mesh) for i in range(n_mesh)])
    summed_prev = lax.ppermute(summed_prev, row, [(i, (i - 1) % n_mesh) for i in range(n_mesh)])
    (grad_mesh,) = call(
        final_kernel,
        [wide],
        [pre_grad, w[3], dst_grad, w[1], new_grad, halo_rows, summed_next, summed_own, summed_prev, w[0]],
        4 * mesh_rows * square,
    )
    grad_biases, grad_gains, grad_weights = call(
        functools.partial(spread_kernel, (6, 7, 8, 2, 3, 4, 5, 0, 1)),
        [((3, features), F32), ((3, features), F32), ((9, features, features), F32)],
        [jnp.stack(places).astype(jnp.int32)] + blocks,
        0,
    )
    return grad_mesh, grad_grid, grad_weights, grad_biases, grad_gains


def solution(mesh):
    n_mesh, n_band = mesh.devices.shape
    side = math.isqrt(n_mesh // 2)
    axes = jax.sharding.Mesh(mesh.devices.reshape(n_mesh // (2 * side), side, 2, n_band), AXES)
    both = P(AXES)
    return jax.shard_map(
        body,
        mesh=axes,
        in_specs=(both, both, P(), P(), P(), both, both, both, both, both, both, P(None, AXES)),
        out_specs=(both, both, P(), P(), P()),
        check_vma=False,
    )
```

```python
import functools
import math

import jax
import jax.numpy as jnp
from jax import lax
from jax.experimental import pallas as pl
from jax.experimental.pallas import tpu as pltpu
from jax.sharding import PartitionSpec as P

EPSILON = 1e-05
BF = jnp.bfloat16
F32 = jnp.float32
LANES = 128
TILE = 16
PIECES = 64
AXES = ("x", "y", "core", "z")
CHIPS = ("x", "y", "z")


def dot(left, right):
    return jnp.dot(left, right, preferred_element_type=F32)


def dot_t(left, right):
    return lax.dot_general(left, right, (((1,), (1,)), ((), ())), preferred_element_type=F32)


def t_dot(left, right):
    return lax.dot_general(left, right, (((0,), (0,)), ((), ())), preferred_element_type=F32)


def sigmoid(value):
    return 0.5 * jnp.tanh(0.5 * value) + 0.5


def row_mean(value):
    return jnp.mean(value, axis=-1, keepdims=True)


def norm_forward(mixed):
    centered = mixed - row_mean(mixed)
    inverse = lax.rsqrt(row_mean(centered * centered) + EPSILON)
    return centered * inverse, inverse


def norm_backward(normed, inverse, scaled):
    return inverse * (scaled - row_mean(scaled) - normed * row_mean(scaled * normed))


def one_hot(mask):
    return jnp.where(mask, 1.0, 0.0).astype(BF)


def as_columns(index):
    return jnp.transpose(index.astype(F32)).astype(jnp.int32)


def pick_matrix(columns, first, blocks, size):
    lanes = lax.broadcasted_iota(jnp.int32, (LANES, size), 1)
    parts = [one_hot(columns[:, b : b + 1] == lanes) for b in range(first, first + blocks)]
    return jnp.concatenate(parts, axis=0)


def place_matrix(rows, first, blocks, size):
    sublanes = lax.broadcasted_iota(jnp.int32, (size, LANES), 0)
    parts = [one_hot(rows[b : b + 1, :] == sublanes) for b in range(first, first + blocks)]
    return jnp.concatenate(parts, axis=1)


class Operand:
    def __init__(self, source, buffer, semaphore):
        self.source, self.buffer, self.semaphore = source, buffer, semaphore
        self.shape, self.dtype = buffer.shape, buffer.dtype
        self.arrived = False

    def copies(self):
        if not isinstance(self.source, list):
            return [pltpu.make_async_copy(self.source, self.buffer, self.semaphore.at[0])]
        size = self.shape[0] // len(self.source)
        return [
            pltpu.make_async_copy(source, self.buffer.at[pl.ds(k * size, size)], self.semaphore.at[k])
            for k, source in enumerate(self.source)
        ]

    def start(self):
        for copy in self.copies():
            copy.start()

    def get(self):
        if not self.arrived:
            for copy in self.copies():
                copy.wait()
            self.arrived = True
        return self.buffer

    def __getitem__(self, index):
        return self.get()[index]


class Stream(Operand):
    def run(self, number):
        count = self.semaphore.shape[0]
        size = self.shape[0] // count
        rows = pl.ds(number * size if isinstance(number, int) else pl.multiple_of(number * size, size), size)
        return pltpu.make_async_copy(self.source.at[rows], self.buffer.at[rows], self.semaphore.at[number])

    def arrive(self, number):
        self.run(number).wait()

    def get(self):
        return self.buffer


class Result:
    def __init__(self, target, buffer, semaphore):
        self.target, self.buffer, self.semaphore = target, buffer, semaphore
        self.shape, self.dtype = buffer.shape, buffer.dtype
        self.sent = False

    def __getitem__(self, index):
        return self.buffer[index]

    def __setitem__(self, index, value):
        self.buffer[index] = value

    def send(self, rows=None):
        self.sent = True
        if rows is None:
            pltpu.make_async_copy(self.buffer, self.target, self.semaphore).start()
        else:
            pltpu.make_async_copy(self.buffer.at[rows], self.target.at[rows], self.semaphore).start()

    def finish(self):
        if not self.sent:
            self.send()
        pltpu.make_async_copy(self.buffer, self.target, self.semaphore).wait()


def call(kernel, outs, args, flops, scratch=(), streams=(), runs=1, after=(), near=()):
    arrays, places, shapes, kinds = [], [], [], []

    def place(array):
        for k, other in enumerate(arrays):
            if other is array:
                return k
        arrays.append(array)
        return len(arrays) - 1

    for arg in args:
        if isinstance(arg, list):
            places.append([place(array) for array in arg])
            shapes.append((len(arg) * arg[0].shape[0],) + arg[0].shape[1:])
            kinds.append(arg[0].dtype)
            continue
        array, entry = arg if isinstance(arg, tuple) else (arg, None)
        places.append((place(array), entry))
        shapes.append(array.shape if entry is None else array.shape[1:])
        kinds.append(array.dtype)
    scalar = [len(shape) == 1 for shape in shapes]
    buffers, semaphores = [], []
    for number, where in enumerate(places):
        if not scalar[number]:
            buffers.append(pltpu.VMEM(shapes[number], kinds[number]))
            count = len(where) if isinstance(where, list) else runs if number in streams else 1
            semaphores.append(pltpu.SemaphoreType.DMA((count,)))
    for array in after:
        place(array)
    out_shapes = [(pltpu.HBM if near else jax.ShapeDtypeStruct)(shape, kind) for shape, kind in outs]
    out_buffers = [pltpu.VMEM(shape, kind) for shape, kind in outs]
    operands = arrays
    n_in, n_out, n_buf = len(operands), len(out_shapes), len(buffers)

    def wrapped(*refs):
        sources, targets = refs[:n_in], refs[n_in : n_in + n_out]
        rest = refs[n_in + n_out :]
        in_buffers, rest = rest[:n_buf], rest[n_buf:]
        out_refs, rest = rest[:n_out], rest[n_out:]
        in_semaphores, rest = rest[:n_buf], rest[n_buf:]
        out_semaphore, user = rest[0], rest[1:]
        inputs, position = [], 0
        for number, where in enumerate(places):
            if scalar[number]:
                inputs.append(sources[where[0]])
                continue
            if isinstance(where, list):
                source = [sources[k] for k in where]
            else:
                source = sources[where[0]] if where[1] is None else sources[where[0]].at[where[1]]
            kind = Stream if number in streams else Operand
            inputs.append(kind(source, in_buffers[position], in_semaphores[position]))
            position += 1
        for item in inputs:
            if isinstance(item, Operand) and not isinstance(item, Stream):
                item.start()
        for number in range(runs if streams else 0):
            for item in inputs:
                if isinstance(item, Stream):
                    item.run(number).start()
        results = []
        for number in range(n_out):
            results.append(Result(targets[number], out_refs[number], out_semaphore.at[number]))
        kernel(*inputs, *results, *user)
        for item in inputs:
            if isinstance(item, Operand) and not isinstance(item, Stream):
                item.get()
        for item in results:
            item.finish()

    moved = sum(math.prod(s) * t.itemsize for s, t in zip(shapes, kinds))
    moved += sum(math.prod(s) * jnp.dtype(t).itemsize for s, t in outs)
    return pl.pallas_call(
        wrapped,
        out_shape=out_shapes,
        in_specs=[pl.BlockSpec(memory_space=pltpu.SMEM if a.ndim == 1 else pl.ANY) for a in operands],
        out_specs=[pl.BlockSpec(memory_space=pl.ANY)] * n_out,
        scratch_shapes=buffers + out_buffers + semaphores + [pltpu.SemaphoreType.DMA((n_out,))] + list(scratch),
        compiler_params=pltpu.CompilerParams(vmem_limit_bytes=(36 if near else 56) * 1024 * 1024),
        cost_estimate=pl.CostEstimate(flops=flops, bytes_accessed=moved, transcendentals=0),
    )(
        *[
            a if a.ndim == 1 or any(a is b for b in near) else pltpu.with_memory_space_constraint(a, pltpu.HBM)
            for a in operands
        ]
    )


def halo_kernel(mesh_ref, index_ref, *out_refs):
    columns = as_columns(index_ref[...])
    for c in (1, 0, 2):
        out_refs[c][...] = dot(pick_matrix(columns, c, 1, mesh_ref.shape[0]), mesh_ref[...]).astype(BF)
        out_refs[c].send()


def diagonal():
    shape = (LANES, LANES)
    return lax.broadcasted_iota(jnp.int32, shape, 0) == lax.broadcasted_iota(jnp.int32, shape, 1)


def column_as_rows(column):
    parts = [column[k : k + LANES] for k in range(0, column.shape[0], LANES)]
    return jnp.concatenate(
        [jnp.sum(jnp.where(diagonal(), part, 0.0), axis=0, keepdims=True) for part in parts], axis=0
    )


def rows_as_column(rows):
    parts = [rows[k : k + 1] for k in range(rows.shape[0])]
    return jnp.concatenate(
        [jnp.sum(jnp.where(diagonal(), part, 0.0), axis=1, keepdims=True) for part in parts], axis=0
    )


def live_rows(index, count):
    blocks = lax.broadcasted_iota(jnp.int32, index.shape, 0)
    return jnp.where(blocks < count, index, -1)


def edge_forward_kernel(
    n_band, count_ref, band_ref, mesh_ref, w1, tables, w0, source_ref, target_ref, biases, w2, w3, w4, w5, w6, gains,
    send_ref, hidden_ref, slope_ref, normed_ref, inverse_ref, aggregate_ref, node_hidden_ref, node_slope_ref,
    node_normed_ref, node_inverse_ref, new_mesh_ref, outbound_ref, table_ref, dst_ref, summed_ref,
):
    mesh_rows = mesh_ref.shape[0]
    size = n_band * LANES
    dst_ref[...] = (dot(mesh_ref[...], w1[...]) + biases[0:1, :]).astype(BF)
    table_ref[...] = dot(tables[...], w0[...]).astype(BF)
    summed_ref[...] = jnp.zeros(summed_ref.shape, F32)
    w2, source_ref, target_ref = w2.get(), source_ref.get(), target_ref.get()

    def group(c, carry):
        source_columns = as_columns((source_ref[c] - band_ref[0] * LANES) & (size - 1))
        targets = live_rows(target_ref[c], count_ref[c])
        target_columns = as_columns(targets)
        table = table_ref[pl.ds(pl.multiple_of(c * size, size), size), :]
        preact = dot(pick_matrix(source_columns, 0, 8, size), table)
        preact += dot(pick_matrix(target_columns, 0, 8, mesh_rows), dst_ref[...])
        gate = sigmoid(preact)
        hidden = (preact * gate).astype(BF)
        normed, inverse = norm_forward(dot(hidden, w2[...]))
        normed = normed.astype(BF)
        rows = pl.ds(pl.multiple_of(c * 8 * LANES, 8 * LANES), 8 * LANES)
        hidden_ref[rows, :] = hidden
        slope_ref[rows, :] = (gate * (1.0 + preact * (1.0 - gate))).astype(BF)
        normed_ref[rows, :] = normed
        inverse_ref[c] = column_as_rows(inverse)
        summed_ref[...] += dot(place_matrix(targets, 0, 8, mesh_rows), normed)
        for out_ref in (hidden_ref, slope_ref, normed_ref):
            out_ref.send(rows)
        return carry

    lax.fori_loop(0, 3, group, 0)
    for out_ref in (hidden_ref, slope_ref, normed_ref):
        out_ref.sent = True
    w3, w4, w5, w6, gains, send_ref = (item.get() for item in (w3, w4, w5, w6, gains, send_ref))
    aggregate = (summed_ref[...] * gains[0:1, :]).astype(BF)
    aggregate_ref[...] = aggregate
    node_pre = dot(mesh_ref[...], w3[...]) + biases[1:2, :] + dot(aggregate, w4[...])
    gate = sigmoid(node_pre)
    node_hidden = (node_pre * gate).astype(BF)
    node_hidden_ref[...] = node_hidden
    node_slope_ref[...] = (gate * (1.0 + node_pre * (1.0 - gate))).astype(BF)
    normed, inverse = norm_forward(dot(node_hidden, w5[...]))
    node_normed_ref[...] = normed.astype(BF)
    node_inverse_ref[...] = column_as_rows(inverse)
    new_mesh = (mesh_ref[...].astype(F32) + normed * gains[1:2, :]).astype(BF)
    new_mesh_ref[...] = new_mesh
    for out_ref in (aggregate_ref, node_hidden_ref, node_slope_ref, node_normed_ref, node_inverse_ref, new_mesh_ref):
        out_ref.send()
    value = dot(new_mesh, w6[...]).astype(BF)
    outbound_ref[...] = dot(pick_matrix(as_columns(send_ref[...]), 0, 8, mesh_rows), value).astype(BF)


def decoder_kernel(
    grid_ref, w7, biases, cot_ref, gains, source_ref, received_ref, w8,
    slot_ref, proj_grad_ref, weight_ref, gain_ref,
):
    slots = received_ref.shape[0]
    rows = grid_ref.shape[0]
    for item in (grid_ref, w7, biases, cot_ref, gains, source_ref, received_ref, w8):
        item.get()
    proj = (dot(grid_ref[...], w7[...]) + biases[2:3, :]).astype(BF).astype(F32)
    cot = cot_ref[...].astype(F32)
    cot = jnp.concatenate([cot] * 3, axis=0)
    preact = dot(pick_matrix(as_columns(source_ref[...]), 0, 12, slots), received_ref[...])
    preact += jnp.concatenate([proj] * 3, axis=0)
    gate = sigmoid(preact)
    hidden = (preact * gate).astype(BF)
    slope = gate * (1.0 + preact * (1.0 - gate))
    normed, inverse = norm_forward(dot(hidden, w8[...]))
    grad_mixed = norm_backward(normed, inverse, cot * gains[2:3, :]).astype(BF)
    gain_ref[...] = jnp.sum(cot * normed, axis=0, keepdims=True)
    grad_pre = (dot_t(grad_mixed, w8[...]) * slope).astype(BF)
    slot_ref[...] = dot(place_matrix(source_ref[...], 0, 12, slots), grad_pre).astype(BF)
    slot_ref.send()
    wide = grad_pre.astype(F32)
    proj_grad_ref[...] = (wide[:rows] + wide[rows : 2 * rows] + wide[2 * rows :]).astype(BF)
    proj_grad_ref.send()
    weight_ref[...] = t_dot(hidden, grad_mixed)


def put_pieces(out_ref, slot, value):
    rounded = value.astype(BF)
    groups = value.shape[0] // TILE
    for h in range(2):
        block = rounded[:, h * LANES : (h + 1) * LANES].reshape(groups, TILE, LANES)
        out_ref[h * groups : (h + 1) * groups, :, slot * LANES : (slot + 1) * LANES] = block


def split_columns(core_ref, size):
    half = size // 2
    mine = core_ref[0] * half
    return pl.ds(pl.multiple_of(mine, half), half), pl.ds(pl.multiple_of(half - mine, half), half)


def put_whole(factor, core_ref, value_ref, keep_ref, send_ref, slot):
    for columns, out_ref in zip(split_columns(core_ref, value_ref.shape[1]), (keep_ref, send_ref)):
        put_pieces(out_ref, slot, value_ref[:, columns] * factor)


def put_outer(factor, core_ref, left_ref, right_ref, keep_ref, send_ref, slot, product_ref):
    product_ref[...] = t_dot(left_ref[...], right_ref[...])
    put_whole(factor, core_ref, product_ref, keep_ref, send_ref, slot)


def grid_kernel(
    factor, core_ref, proj_grad_ref, grid_ref, dec_weight, cot_ref, w7, keep_ref, send_ref, grad_ref, bias_ref,
    product_ref,
):
    put_outer(factor, core_ref, grid_ref, proj_grad_ref, keep_ref, send_ref, 0, product_ref)
    put_whole(factor, core_ref, dec_weight, keep_ref, send_ref, 1)
    keep_ref.send()
    send_ref.send()
    proj_grad = proj_grad_ref[...]
    grad_ref[...] = (cot_ref[...].astype(F32) + dot_t(proj_grad, w7[...])).astype(BF)
    grad_ref.send()
    bias_ref[...] = jnp.sum(proj_grad.astype(F32), axis=0, keepdims=True)


def node_backward_kernel(
    factor, core_ref, send_ref, returned_ref, w6, node_normed_ref, node_inverse_ref, gains, w5, node_slope_ref, w4,
    aggregate_ref, mesh_ref, node_hidden_ref, new_mesh_ref,
    new_grad_ref, pre_grad_ref, scaled_ref, gain_ref, out_keep, out_send, value_grad_ref, out_grad_ref,
    product_ref,
):
    mesh_rows = node_normed_ref.shape[0]
    value_grad = dot(place_matrix(send_ref[...], 0, 8, mesh_rows), returned_ref[...]).astype(BF)
    value_grad_ref[...] = value_grad
    new_grad = dot_t(value_grad, w6[...])
    new_grad_ref[...] = new_grad
    normed = node_normed_ref[...].astype(F32)
    inverse = rows_as_column(node_inverse_ref[...])
    out_grad = norm_backward(normed, inverse, new_grad * gains[1:2, :]).astype(BF)
    out_grad_ref[...] = out_grad
    pre_grad = (dot_t(out_grad, w5[...]) * node_slope_ref[...].astype(F32)).astype(BF)
    pre_grad_ref[...] = pre_grad
    aggregate_grad = dot_t(pre_grad, w4[...])
    scaled_ref[...] = (aggregate_grad * gains[0:1, :]).astype(BF)
    summed = aggregate_ref[...].astype(F32)
    gain_ref[0:1, :] = jnp.sum(aggregate_grad * summed, axis=0, keepdims=True) / gains[0:1, :]
    gain_ref[1:2, :] = jnp.sum(new_grad * normed, axis=0, keepdims=True)
    for item in (new_grad_ref, pre_grad_ref, scaled_ref):
        item.send()
    put_outer(factor, core_ref, mesh_ref, pre_grad_ref, out_keep, out_send, 0, product_ref)
    put_outer(factor, core_ref, aggregate_ref, pre_grad_ref, out_keep, out_send, 1, product_ref)
    put_outer(factor, core_ref, node_hidden_ref, out_grad_ref, out_keep, out_send, 2, product_ref)
    put_outer(factor, core_ref, new_mesh_ref, value_grad_ref, out_keep, out_send, 3, product_ref)


def share_kernel(chips, *refs):
    out_ref = refs[-1]
    own = PIECES // chips
    first = 0
    for got_ref in refs[:-1]:
        got_ref = got_ref.get()
        width = got_ref.shape[2]
        total = got_ref[0:own].astype(F32)
        for k in range(1, chips):
            total += got_ref[k * own : (k + 1) * own].astype(F32)
        rounded = total.astype(BF)
        for copy in range(out_ref.shape[0]):
            out_ref[copy, :, :, first : first + width] = rounded
        first += width


def spread_kernel(slots, core_ref, mine_ref, other_ref, biases_ref, gains_ref, out_ref):
    groups = out_ref.shape[1] // TILE
    count = len(slots)
    mine_ref, other_ref = mine_ref.get(), other_ref.get()
    for entry in range(-1, count):
        slot = slots[entry] if entry >= 0 else count
        for start, block_ref in ((core_ref[0] * 2, mine_ref), (2 - core_ref[0] * 2, other_ref)):
            for h in range(2):
                columns = pl.ds(pl.multiple_of((start + h) * LANES, LANES), LANES)
                lanes = slice(slot * LANES, (slot + 1) * LANES)
                if entry < 0:
                    value = block_ref[h * groups, :, lanes].astype(F32)
                    biases_ref[:, columns] = value[0:3]
                    gains_ref[:, columns] = value[3:6]
                else:
                    value = block_ref[h * groups : (h + 1) * groups, :, lanes]
                    out_ref[entry, :, columns] = value.reshape(groups * TILE, LANES).astype(F32)
        if entry >= 0:
            out_ref.send(pl.ds(entry, 1))


def edge_backward_kernel(
    factor, n_band, count_ref, core_ref, band_ref, source_ref, target_ref, scaled_ref, w2, inverse_ref, normed_ref,
    hidden_ref, slope_ref, mesh_ref, tables, pre_grad_ref, grid_bias_ref, gains_ref, dec_gain_ref,
    table_ref, dst_ref, keep_ref, send_ref, dst_sum, weight_sum, small_sum, right_ref,
):
    mesh_rows = scaled_ref.shape[0]
    size = n_band * LANES
    dst_sum[...] = jnp.zeros(dst_sum.shape, F32)
    weight_sum[...] = jnp.zeros(weight_sum.shape, F32)
    scaled_ref, w2, source_ref, target_ref, inverse_ref = (
        item.get() for item in (scaled_ref, w2, source_ref, target_ref, inverse_ref)
    )

    def group(c, carry):
        for item in (normed_ref, hidden_ref, slope_ref):
            item.arrive(c)
        targets = live_rows(target_ref[c], count_ref[c])
        rows = pl.ds(pl.multiple_of(c * 8 * LANES, 8 * LANES), 8 * LANES)
        scaled = dot(pick_matrix(as_columns(targets), 0, 8, mesh_rows), scaled_ref[...])
        inverse = rows_as_column(inverse_ref[c])
        grad_mixed = norm_backward(normed_ref[rows, :].astype(F32), inverse, scaled).astype(BF)
        weight_sum[...] += t_dot(hidden_ref[rows, :], grad_mixed)
        grad_pre = (dot_t(grad_mixed, w2[...]) * slope_ref[rows, :].astype(F32)).astype(BF)
        dst_sum[...] += dot(place_matrix(targets, 0, 8, mesh_rows), grad_pre)
        placed = dot(place_matrix(source_ref[c], 0, 8, size), grad_pre).astype(BF)
        for j in range(n_band):
            table_ref[j, c] = placed[j * LANES : (j + 1) * LANES, :]
            there = lax.rem(j + n_band - band_ref[0], n_band)
            right_ref[pl.ds(pl.multiple_of((c * n_band + there) * LANES, LANES), LANES), :] = placed[
                j * LANES : (j + 1) * LANES, :
            ]
        return carry

    lax.fori_loop(0, 3, group, 0)
    table_ref.send()
    dst_grad = dst_sum[...].astype(BF)
    dst_ref[...] = dst_grad
    dst_ref.send()
    put_whole(factor, core_ref, weight_sum, keep_ref, send_ref, 2)
    put_outer(factor, core_ref, tables, right_ref, keep_ref, send_ref, 0, small_sum)
    put_outer(factor, core_ref, mesh_ref, dst_ref, keep_ref, send_ref, 1, weight_sum)
    small_sum[...] = jnp.zeros(small_sum.shape, F32)
    small_sum[0:1, :] = jnp.sum(dst_grad.astype(F32), axis=0, keepdims=True)
    small_sum[1:2, :] = jnp.sum(pre_grad_ref[...].astype(F32), axis=0, keepdims=True)
    small_sum[2:3, :] = grid_bias_ref[...]
    small_sum[3:5, :] = gains_ref[...]
    small_sum[5:6, :] = dec_gain_ref[...]
    put_whole(factor, core_ref, small_sum, keep_ref, send_ref, 3)


def band_sum_kernel(*refs):
    blocks, outs = refs[:-3], refs[-3:]
    for c in (0, 2, 1):
        total = blocks[0][c].astype(F32)
        for block_ref in blocks[1:]:
            total += block_ref[c].astype(F32)
        outs[c][...] = total.astype(BF)
        outs[c].send()


def final_kernel(
    pre_grad_ref, w3, dst_grad_ref, w1, new_grad_ref, index_ref, next_ref, own_ref, prev_ref, w0, grad_ref
):
    mesh_rows = new_grad_ref.shape[0]
    partial = new_grad_ref[...] + dot_t(pre_grad_ref[...], w3[...]) + dot_t(dst_grad_ref[...], w1[...])
    halo = jnp.concatenate([next_ref[...], own_ref[...], prev_ref[...]], axis=0)
    src_grad = dot(place_matrix(index_ref[...], 0, 3, mesh_rows), halo)
    grad_ref[...] = (partial + dot_t(src_grad.astype(BF), w0[...])).astype(BF)


def routes(n_mesh, n_band):
    found = {}
    for c in range(3):
        for step in range(n_band):
            if c == 1 and step == 0:
                continue
            found[c, step] = [
                (((i - c + 1) % n_mesh) * n_band + (j + step) % n_band, i * n_band + j)
                for i in range(n_mesh)
                for j in range(n_band)
            ]
    return found


def swap(value):
    return lax.ppermute(value, "core", [(0, 1), (1, 0)])


def pair(keep, got):
    return (keep.astype(F32) + got.astype(F32)).astype(BF)


def pad_rows(index, rows):
    return jnp.pad(index, ((0, rows - index.shape[0]), (0, 0)))


def body(
    mesh_latent, grid_latent, weights, biases, gains, cotangent, halo_index, edge_source, edge_target,
    block_count, decoder_send, decoder_source,
):
    n_band = lax.axis_size("z")
    n_mesh = lax.axis_size(("x", "y", "core"))
    n_x, plane = lax.axis_size("x"), lax.axis_size(("y", "z"))
    chips = n_x * plane
    own = PIECES // chips
    mesh_rows, features = mesh_latent.shape
    grid_rows = grid_latent.shape[0]
    shards, slots_each = decoder_send.shape[1:]
    slots = shards * slots_each
    edges = 3 * edge_source.shape[2] * edge_source.shape[3]
    square = 2 * features * features
    factor = 1.0 / math.sqrt(grid_rows * n_mesh * n_band)
    w = [(weights, k) for k in range(9)]
    paths = routes(n_mesh, n_band)
    core, band = lax.axis_index("core"), lax.axis_index("z")
    core_row, band_row = core[None], band[None]
    sources, targets, counts = edge_source[0], edge_target[0], block_count[0]
    wide, wide32 = ((mesh_rows, features), BF), ((mesh_rows, features), F32)
    block = ((LANES, features), BF)

    def half(count):
        return [((PIECES, TILE, count * LANES), BF)] * 2

    halo_rows = pad_rows(halo_index[0], 8)
    outgoing = call(halo_kernel, [block] * 3, [mesh_latent, halo_rows], 384 * square)
    tables = []
    for c in range(3):
        for step in range(n_band):
            tables.append(lax.ppermute(outgoing[c], AXES, paths[c, step]) if (c, step) in paths else outgoing[c])

    send_rows = decoder_send[0].reshape(slots // LANES, LANES)
    source_rows = pad_rows(decoder_source.reshape(3 * grid_rows // LANES, LANES), 16)
    small_inverse = ((mesh_rows // LANES, LANES), F32)
    (
        hidden, slope, normed, inverse, aggregate, node_hidden, node_slope, node_normed, node_inverse, new_mesh, outbound,
    ) = call(
        functools.partial(edge_forward_kernel, n_band),
        [
            ((edges, features), BF), ((edges, features), BF), ((edges, features), BF), (targets.shape, F32),
            wide, wide, wide, wide, small_inverse, wide, ((slots, features), BF),
        ],
        [counts, band_row, mesh_latent, w[1], tables]
        + [w[0], sources, targets, biases, w[2], w[3], w[4], w[5], w[6], gains, send_rows],
        5 * edges * square,
        [
            pltpu.VMEM((3 * n_band * LANES, features), BF), pltpu.VMEM((mesh_rows, features), BF),
            pltpu.VMEM((mesh_rows, features), F32),
        ],
    )
    received = lax.all_to_all(
        outbound.reshape(shards, slots_each, features), AXES, split_axis=0, concat_axis=0, tiled=True
    ).reshape(slots, features)
    slot_grad, proj_grad, dec_weight, dec_gain = call(
        decoder_kernel,
        [((slots, features), BF), ((grid_rows, features), BF), ((features, features), F32), ((1, features), F32)],
        [grid_latent, w[7], biases, cotangent, gains, source_rows, received, w[8]],
        7 * 3 * grid_rows * square,
        near=[received],
    )
    returned = lax.all_to_all(
        slot_grad.reshape(shards, slots_each, features), AXES, split_axis=0, concat_axis=0, tiled=True
    ).reshape(slots, features)
    late_keep, late_send, grad_grid, grid_bias = call(
        functools.partial(grid_kernel, factor),
        half(2) + [((grid_rows, features), BF), ((1, features), F32)],
        [core_row, proj_grad, grid_latent, dec_weight, cotangent, w[7]],
        2 * grid_rows * square,
        [pltpu.VMEM((features, features), F32)],
    )
    late_got = swap(late_send)
    returned, late_keep, late_got = lax.optimization_barrier((returned, late_keep, late_got))
    new_grad, pre_grad, scaled, node_gains, node_keep, node_send = call(
        functools.partial(node_backward_kernel, factor),
        [wide32, wide, wide, ((2, features), F32)] + half(4),
        [
            core_row, send_rows, returned, w[6], node_normed, node_inverse, gains, w[5], node_slope, w[4],
            aggregate, mesh_latent, node_hidden, new_mesh,
        ],
        9 * mesh_rows * square,
        [
            pltpu.VMEM((mesh_rows, features), BF), pltpu.VMEM((mesh_rows, features), BF),
            pltpu.VMEM((features, features), F32),
        ],
        near=[returned],
    )
    early = jnp.concatenate([pair(late_keep, late_got), pair(node_keep, swap(node_send))], axis=2)
    early = lax.all_to_all(early, CHIPS, split_axis=0, concat_axis=0, tiled=True)
    square_shape = (features, features)
    table_grad, dst_grad, edge_keep, edge_send = call(
        functools.partial(edge_backward_kernel, factor, n_band),
        [((n_band, 3, LANES, features), BF), wide] + half(4),
        [
            counts, core_row, band_row, sources, targets, scaled, w[2], inverse, normed, hidden, slope, mesh_latent,
            tables, pre_grad, grid_bias, node_gains, dec_gain,
        ],
        7 * edges * square,
        [
            pltpu.VMEM((mesh_rows, features), F32), pltpu.VMEM(square_shape, F32), pltpu.VMEM(square_shape, F32),
            pltpu.VMEM((3 * n_band * LANES, features), BF),
        ],
        streams=(8, 9, 10),
        runs=3,
    )
    edge_got = swap(edge_send)
    edge_got, _ = lax.optimization_barrier((edge_got, early))
    late = pair(edge_keep, edge_got)
    late = lax.all_to_all(late, CHIPS, split_axis=0, concat_axis=0, tiled=True)
    (shared,) = call(
        functools.partial(share_kernel, chips), [((plane, own, TILE, 10 * LANES), BF)], [early, late], 0, near=[early, late]
    )
    block_rows = lax.all_to_all(shared, ("y", "z"), split_axis=0, concat_axis=0, tiled=True)
    block_rows = block_rows.reshape(plane * own, TILE, 10 * LANES)
    table_grad, _ = lax.optimization_barrier((table_grad, shared))
    swept = []
    for step in range(n_band):
        piece = lax.dynamic_index_in_dim(table_grad, lax.rem(band + step, n_band), 0, keepdims=False)
        swept.append(
            lax.ppermute(piece, "z", [(i, (i + step) % n_band) for i in range(n_band)]) if step else piece
        )
    mine = jnp.broadcast_to(block_rows[None], (n_x,) + block_rows.shape)
    mine = lax.all_to_all(mine, "x", split_axis=0, concat_axis=0, tiled=True)
    mine = mine.reshape(PIECES, TILE, 10 * LANES)
    summed_next, summed_own, summed_prev = call(band_sum_kernel, [block] * 3, swept, 0)
    row = ("x", "y", "core")
    summed_next = lax.ppermute(summed_next, row, [(i, (i + 1) % n_mesh) for i in range(n_mesh)])
    summed_prev = lax.ppermute(summed_prev, row, [(i, (i - 1) % n_mesh) for i in range(n_mesh)])
    mine, _, _ = lax.optimization_barrier((mine, summed_next, summed_prev))
    other = swap(mine)
    (grad_mesh,) = call(
        final_kernel,
        [wide],
        [pre_grad, w[3], dst_grad, w[1], new_grad, halo_rows, summed_next, summed_own, summed_prev, w[0]],
        4 * mesh_rows * square,
    )
    grad_biases, grad_gains, grad_weights = call(
        functools.partial(spread_kernel, (6, 7, 8, 2, 3, 4, 5, 0, 1)),
        [((3, features), F32), ((3, features), F32), ((9, features, features), F32)],
        [core_row, mine, other],
        0,
        after=[grad_mesh],
        near=[mine, other],
    )
    return grad_mesh, grad_grid, grad_weights, grad_biases, grad_gains


def solution(mesh):
    n_mesh, n_band = mesh.devices.shape
    side = math.isqrt(n_mesh // 2)
    axes = jax.sharding.Mesh(mesh.devices.reshape(n_mesh // (2 * side), side, 2, n_band), AXES)
    both = P(AXES)
    return jax.shard_map(
        body,
        mesh=axes,
        in_specs=(both, both, P(), P(), P(), both, both, both, both, both, both, P(None, AXES)),
        out_specs=(both, both, P(), P(), P()),
        check_vma=False,
    )
```

```python
import functools
import math

import jax
import jax.numpy as jnp
from jax import lax
from jax.experimental import pallas as pl
from jax.experimental.pallas import tpu as pltpu
from jax.sharding import PartitionSpec as P

EPSILON = 1e-05
BF = jnp.bfloat16
F32 = jnp.float32
LANES = 128
TILE = 16
PIECES = 64
AXES = ("x", "y", "core", "z")
CHIPS = ("x", "y", "z")


def dot(left, right):
    return jnp.dot(left, right, preferred_element_type=F32)


def dot_t(left, right):
    return lax.dot_general(left, right, (((1,), (1,)), ((), ())), preferred_element_type=F32)


def t_dot(left, right):
    return lax.dot_general(left, right, (((0,), (0,)), ((), ())), preferred_element_type=F32)


def sigmoid(value):
    return 0.5 * jnp.tanh(0.5 * value) + 0.5


def row_mean(value):
    return jnp.mean(value, axis=-1, keepdims=True)


def norm_forward(mixed):
    centered = mixed - row_mean(mixed)
    inverse = lax.rsqrt(row_mean(centered * centered) + EPSILON)
    return centered * inverse, inverse


def norm_backward(normed, inverse, scaled):
    return inverse * (scaled - row_mean(scaled) - normed * row_mean(scaled * normed))


def one_hot(mask):
    return jnp.where(mask, 1.0, 0.0).astype(BF)


def as_columns(index):
    return jnp.transpose(index.astype(F32)).astype(jnp.int32)


def pick_matrix(columns, first, blocks, size):
    lanes = lax.broadcasted_iota(jnp.int32, (LANES, size), 1)
    parts = [one_hot(columns[:, b : b + 1] == lanes) for b in range(first, first + blocks)]
    return jnp.concatenate(parts, axis=0)


def place_matrix(rows, first, blocks, size):
    sublanes = lax.broadcasted_iota(jnp.int32, (size, LANES), 0)
    parts = [one_hot(rows[b : b + 1, :] == sublanes) for b in range(first, first + blocks)]
    return jnp.concatenate(parts, axis=1)


class Operand:
    def __init__(self, source, buffer, semaphore):
        self.source, self.buffer, self.semaphore = source, buffer, semaphore
        self.shape, self.dtype = buffer.shape, buffer.dtype
        self.arrived = False

    def copies(self):
        if not isinstance(self.source, list):
            return [pltpu.make_async_copy(self.source, self.buffer, self.semaphore.at[0])]
        size = self.shape[0] // len(self.source)
        return [
            pltpu.make_async_copy(source, self.buffer.at[pl.ds(k * size, size)], self.semaphore.at[k])
            for k, source in enumerate(self.source)
        ]

    def start(self):
        for copy in self.copies():
            copy.start()

    def get(self):
        if not self.arrived:
            for copy in self.copies():
                copy.wait()
            self.arrived = True
        return self.buffer

    def __getitem__(self, index):
        return self.get()[index]


class Stream(Operand):
    def run(self, number):
        count = self.semaphore.shape[0]
        size = self.shape[0] // count
        rows = pl.ds(number * size if isinstance(number, int) else pl.multiple_of(number * size, size), size)
        return pltpu.make_async_copy(self.source.at[rows], self.buffer.at[rows], self.semaphore.at[number])

    def arrive(self, number):
        self.run(number).wait()

    def get(self):
        return self.buffer


class Result:
    def __init__(self, target, buffer, semaphore):
        self.target, self.buffer, self.semaphore = target, buffer, semaphore
        self.shape, self.dtype = buffer.shape, buffer.dtype
        self.sent = False

    def __getitem__(self, index):
        return self.buffer[index]

    def __setitem__(self, index, value):
        self.buffer[index] = value

    def send(self, rows=None):
        self.sent = True
        if rows is None:
            pltpu.make_async_copy(self.buffer, self.target, self.semaphore).start()
        else:
            pltpu.make_async_copy(self.buffer.at[rows], self.target.at[rows], self.semaphore).start()

    def finish(self):
        if not self.sent:
            self.send()
        pltpu.make_async_copy(self.buffer, self.target, self.semaphore).wait()


def call(kernel, outs, args, flops, scratch=(), streams=(), runs=1, after=(), near=(), loose=()):
    arrays, places, shapes, kinds = [], [], [], []

    def place(array):
        for k, other in enumerate(arrays):
            if other is array:
                return k
        arrays.append(array)
        return len(arrays) - 1

    for arg in args:
        if isinstance(arg, list):
            places.append([(place(array), start) for array, start in arg])
            shapes.append((len(arg) * LANES,) + arg[0][0].shape[1:])
            kinds.append(arg[0][0].dtype)
            continue
        array, entry = arg if isinstance(arg, tuple) else (arg, None)
        places.append((place(array), entry))
        shapes.append(array.shape if entry is None else array.shape[1:])
        kinds.append(array.dtype)
    scalar = [len(shape) == 1 for shape in shapes]
    buffers, semaphores = [], []
    for number, where in enumerate(places):
        if not scalar[number]:
            buffers.append(pltpu.VMEM(shapes[number], kinds[number]))
            count = len(where) if isinstance(where, list) else runs if number in streams else 1
            semaphores.append(pltpu.SemaphoreType.DMA((count,)))
    for array in after:
        place(array)
    out_shapes = [
        (pltpu.HBM if near and number not in loose else jax.ShapeDtypeStruct)(shape, kind)
        for number, (shape, kind) in enumerate(outs)
    ]
    out_buffers = [pltpu.VMEM(shape, kind) for shape, kind in outs]
    operands = arrays
    n_in, n_out, n_buf = len(operands), len(out_shapes), len(buffers)

    def wrapped(*refs):
        sources, targets = refs[:n_in], refs[n_in : n_in + n_out]
        rest = refs[n_in + n_out :]
        in_buffers, rest = rest[:n_buf], rest[n_buf:]
        out_refs, rest = rest[:n_out], rest[n_out:]
        in_semaphores, rest = rest[:n_buf], rest[n_buf:]
        out_semaphore, user = rest[0], rest[1:]
        inputs, position = [], 0
        for number, where in enumerate(places):
            if scalar[number]:
                inputs.append(sources[where[0]])
                continue
            if isinstance(where, list):
                source = [sources[k].at[pl.ds(start, LANES)] for k, start in where]
            else:
                source = sources[where[0]] if where[1] is None else sources[where[0]].at[where[1]]
            kind = Stream if number in streams else Operand
            inputs.append(kind(source, in_buffers[position], in_semaphores[position]))
            position += 1
        for item in inputs:
            if isinstance(item, Operand) and not isinstance(item, Stream):
                item.start()
        for number in range(runs if streams else 0):
            for item in inputs:
                if isinstance(item, Stream):
                    item.run(number).start()
        results = []
        for number in range(n_out):
            results.append(Result(targets[number], out_refs[number], out_semaphore.at[number]))
        kernel(*inputs, *results, *user)
        for item in inputs:
            if isinstance(item, Operand) and not isinstance(item, Stream):
                item.get()
        for item in results:
            item.finish()

    moved = sum(math.prod(s) * t.itemsize for s, t in zip(shapes, kinds))
    moved += sum(math.prod(s) * jnp.dtype(t).itemsize for s, t in outs)
    return pl.pallas_call(
        wrapped,
        out_shape=out_shapes,
        in_specs=[pl.BlockSpec(memory_space=pltpu.SMEM if a.ndim == 1 else pl.ANY) for a in operands],
        out_specs=[pl.BlockSpec(memory_space=pl.ANY)] * n_out,
        scratch_shapes=buffers + out_buffers + semaphores + [pltpu.SemaphoreType.DMA((n_out,))] + list(scratch),
        compiler_params=pltpu.CompilerParams(vmem_limit_bytes=(36 if near else 56) * 1024 * 1024),
        cost_estimate=pl.CostEstimate(flops=flops, bytes_accessed=moved, transcendentals=0),
    )(
        *[
            a if a.ndim == 1 or any(a is b for b in near) else pltpu.with_memory_space_constraint(a, pltpu.HBM)
            for a in operands
        ]
    )


def halo_kernel(mesh_ref, index_ref, *out_refs):
    index = index_ref[...]
    for c in (1, 0, 2):
        out_refs[c][...] = t_dot(place_matrix(index, c, 1, mesh_ref.shape[0]), mesh_ref[...]).astype(BF)
        out_refs[c].send()


def diagonal():
    shape = (LANES, LANES)
    return lax.broadcasted_iota(jnp.int32, shape, 0) == lax.broadcasted_iota(jnp.int32, shape, 1)


def column_as_rows(column):
    parts = [column[k : k + LANES] for k in range(0, column.shape[0], LANES)]
    return jnp.concatenate(
        [jnp.sum(jnp.where(diagonal(), part, 0.0), axis=0, keepdims=True) for part in parts], axis=0
    )


def rows_as_column(rows):
    parts = [rows[k : k + 1] for k in range(rows.shape[0])]
    return jnp.concatenate(
        [jnp.sum(jnp.where(diagonal(), part, 0.0), axis=1, keepdims=True) for part in parts], axis=0
    )


def live_rows(index, count):
    blocks = lax.broadcasted_iota(jnp.int32, index.shape, 0)
    return jnp.where(blocks < count, index, -1)


def edge_forward_kernel(
    n_band, count_ref, band_ref, mesh_ref, w1, tables, w0, source_ref, target_ref, biases, w2, w3, w4, w5, w6, gains,
    send_ref, hidden_ref, slope_ref, normed_ref, inverse_ref, aggregate_ref, node_hidden_ref, node_slope_ref,
    node_normed_ref, node_inverse_ref, new_mesh_ref, outbound_ref, table_ref, dst_ref, summed_ref,
):
    mesh_rows = mesh_ref.shape[0]
    size = n_band * LANES
    dst_ref[...] = (dot(mesh_ref[...], w1[...]) + biases[0:1, :]).astype(BF)
    table_ref[...] = dot(tables[...], w0[...]).astype(BF)
    summed_ref[...] = jnp.zeros(summed_ref.shape, F32)
    w2, source_ref, target_ref = w2.get(), source_ref.get(), target_ref.get()

    def group(c, carry):
        source_columns = as_columns((source_ref[c] - band_ref[0] * LANES) & (size - 1))
        targets = live_rows(target_ref[c], count_ref[c])
        target_columns = as_columns(targets)
        table = table_ref[pl.ds(pl.multiple_of(c * size, size), size), :]
        preact = dot(pick_matrix(source_columns, 0, 8, size), table)
        preact += dot(pick_matrix(target_columns, 0, 8, mesh_rows), dst_ref[...])
        gate = sigmoid(preact)
        hidden = (preact * gate).astype(BF)
        normed, inverse = norm_forward(dot(hidden, w2[...]))
        normed = normed.astype(BF)
        rows = pl.ds(pl.multiple_of(c * 8 * LANES, 8 * LANES), 8 * LANES)
        hidden_ref[rows, :] = hidden
        slope_ref[rows, :] = (gate * (1.0 + preact * (1.0 - gate))).astype(BF)
        normed_ref[rows, :] = normed
        inverse_ref[c] = column_as_rows(inverse)
        summed_ref[...] += dot(place_matrix(targets, 0, 8, mesh_rows), normed)
        for out_ref in (hidden_ref, slope_ref, normed_ref):
            out_ref.send(rows)
        return carry

    lax.fori_loop(0, 3, group, 0)
    for out_ref in (hidden_ref, slope_ref, normed_ref):
        out_ref.sent = True
    w3, w4, w5, w6, gains, send_ref = (item.get() for item in (w3, w4, w5, w6, gains, send_ref))
    aggregate = (summed_ref[...] * gains[0:1, :]).astype(BF)
    aggregate_ref[...] = aggregate
    node_pre = dot(mesh_ref[...], w3[...]) + biases[1:2, :] + dot(aggregate, w4[...])
    gate = sigmoid(node_pre)
    node_hidden = (node_pre * gate).astype(BF)
    node_hidden_ref[...] = node_hidden
    node_slope_ref[...] = (gate * (1.0 + node_pre * (1.0 - gate))).astype(BF)
    normed, inverse = norm_forward(dot(node_hidden, w5[...]))
    node_normed_ref[...] = normed.astype(BF)
    node_inverse_ref[...] = column_as_rows(inverse)
    new_mesh = (mesh_ref[...].astype(F32) + normed * gains[1:2, :]).astype(BF)
    new_mesh_ref[...] = new_mesh
    for out_ref in (aggregate_ref, node_hidden_ref, node_slope_ref, node_normed_ref, node_inverse_ref, new_mesh_ref):
        out_ref.send()
    value = dot(new_mesh, w6[...]).astype(BF)
    outbound_ref[...] = dot(pick_matrix(as_columns(send_ref[...]), 0, 8, mesh_rows), value).astype(BF)


def decoder_kernel(
    grid_ref, w7, biases, cot_ref, gains, source_ref, received_ref, w8,
    slot_ref, proj_grad_ref, weight_ref, gain_ref,
):
    slots = received_ref.shape[0]
    rows = grid_ref.shape[0]
    for item in (grid_ref, w7, biases, cot_ref, gains, source_ref, received_ref, w8):
        item.get()
    proj = (dot(grid_ref[...], w7[...]) + biases[2:3, :]).astype(BF).astype(F32)
    cot = cot_ref[...].astype(F32)
    cot = jnp.concatenate([cot] * 3, axis=0)
    preact = dot(pick_matrix(as_columns(source_ref[...]), 0, 12, slots), received_ref[...])
    preact += jnp.concatenate([proj] * 3, axis=0)
    gate = sigmoid(preact)
    hidden = (preact * gate).astype(BF)
    slope = gate * (1.0 + preact * (1.0 - gate))
    normed, inverse = norm_forward(dot(hidden, w8[...]))
    grad_mixed = norm_backward(normed, inverse, cot * gains[2:3, :]).astype(BF)
    gain_ref[...] = jnp.sum(cot * normed, axis=0, keepdims=True)
    grad_pre = (dot_t(grad_mixed, w8[...]) * slope).astype(BF)
    slot_ref[...] = dot(place_matrix(source_ref[...], 0, 12, slots), grad_pre).astype(BF)
    slot_ref.send()
    wide = grad_pre.astype(F32)
    proj_grad_ref[...] = (wide[:rows] + wide[rows : 2 * rows] + wide[2 * rows :]).astype(BF)
    proj_grad_ref.send()
    weight_ref[...] = t_dot(hidden, grad_mixed)


def put_pieces(out_ref, slot, value):
    rounded = value.astype(BF)
    groups = value.shape[0] // TILE
    for h in range(2):
        block = rounded[:, h * LANES : (h + 1) * LANES].reshape(groups, TILE, LANES)
        out_ref[h * groups : (h + 1) * groups, :, slot * LANES : (slot + 1) * LANES] = block


def split_columns(core_ref, size):
    half = size // 2
    mine = core_ref[0] * half
    return pl.ds(pl.multiple_of(mine, half), half), pl.ds(pl.multiple_of(half - mine, half), half)


def put_whole(factor, core_ref, value_ref, keep_ref, send_ref, slot):
    for columns, out_ref in zip(split_columns(core_ref, value_ref.shape[1]), (keep_ref, send_ref)):
        put_pieces(out_ref, slot, value_ref[:, columns] * factor)


def put_outer(factor, core_ref, left_ref, right_ref, keep_ref, send_ref, slot, product_ref):
    product_ref[...] = t_dot(left_ref[...], right_ref[...])
    put_whole(factor, core_ref, product_ref, keep_ref, send_ref, slot)


def grid_kernel(
    factor, core_ref, proj_grad_ref, grid_ref, dec_weight, cot_ref, w7, keep_ref, send_ref, grad_ref, bias_ref,
    product_ref,
):
    put_outer(factor, core_ref, grid_ref, proj_grad_ref, keep_ref, send_ref, 0, product_ref)
    put_whole(factor, core_ref, dec_weight, keep_ref, send_ref, 1)
    keep_ref.send()
    send_ref.send()
    proj_grad = proj_grad_ref[...]
    grad_ref[...] = (cot_ref[...].astype(F32) + dot_t(proj_grad, w7[...])).astype(BF)
    grad_ref.send()
    bias_ref[...] = jnp.sum(proj_grad.astype(F32), axis=0, keepdims=True)


def node_backward_kernel(
    factor, core_ref, send_ref, returned_ref, w6, node_normed_ref, node_inverse_ref, gains, w5, node_slope_ref, w4,
    aggregate_ref, mesh_ref, node_hidden_ref, new_mesh_ref,
    new_grad_ref, pre_grad_ref, scaled_ref, gain_ref, out_keep, out_send, value_grad_ref, out_grad_ref,
    product_ref,
):
    mesh_rows = node_normed_ref.shape[0]
    value_grad = dot(place_matrix(send_ref[...], 0, 8, mesh_rows), returned_ref[...]).astype(BF)
    value_grad_ref[...] = value_grad
    new_grad = dot_t(value_grad, w6[...])
    new_grad_ref[...] = new_grad
    normed = node_normed_ref[...].astype(F32)
    inverse = rows_as_column(node_inverse_ref[...])
    out_grad = norm_backward(normed, inverse, new_grad * gains[1:2, :]).astype(BF)
    out_grad_ref[...] = out_grad
    pre_grad = (dot_t(out_grad, w5[...]) * node_slope_ref[...].astype(F32)).astype(BF)
    pre_grad_ref[...] = pre_grad
    aggregate_grad = dot_t(pre_grad, w4[...])
    scaled_ref[...] = (aggregate_grad * gains[0:1, :]).astype(BF)
    summed = aggregate_ref[...].astype(F32)
    gain_ref[0:1, :] = jnp.sum(aggregate_grad * summed, axis=0, keepdims=True) / gains[0:1, :]
    gain_ref[1:2, :] = jnp.sum(new_grad * normed, axis=0, keepdims=True)
    for item in (new_grad_ref, pre_grad_ref, scaled_ref):
        item.send()
    put_outer(factor, core_ref, mesh_ref, pre_grad_ref, out_keep, out_send, 0, product_ref)
    put_outer(factor, core_ref, aggregate_ref, pre_grad_ref, out_keep, out_send, 1, product_ref)
    put_outer(factor, core_ref, node_hidden_ref, out_grad_ref, out_keep, out_send, 2, product_ref)
    put_outer(factor, core_ref, new_mesh_ref, value_grad_ref, out_keep, out_send, 3, product_ref)


def share_kernel(chips, *refs):
    out_ref = refs[-1]
    own = PIECES // chips
    first = 0
    for got_ref in refs[:-1]:
        got_ref = got_ref.get()
        width = got_ref.shape[2]
        total = got_ref[0:own].astype(F32)
        for k in range(1, chips):
            total += got_ref[k * own : (k + 1) * own].astype(F32)
        rounded = total.astype(BF)
        for copy in range(out_ref.shape[0]):
            out_ref[copy, :, :, first : first + width] = rounded
        first += width


def spread_kernel(slots, core_ref, mine_ref, other_ref, biases_ref, gains_ref, out_ref):
    groups = out_ref.shape[1] // TILE
    count = len(slots)
    mine_ref, other_ref = mine_ref.get(), other_ref.get()
    for entry in range(-1, count):
        slot = slots[entry] if entry >= 0 else count
        for start, block_ref in ((core_ref[0] * 2, mine_ref), (2 - core_ref[0] * 2, other_ref)):
            for h in range(2):
                columns = pl.ds(pl.multiple_of((start + h) * LANES, LANES), LANES)
                lanes = slice(slot * LANES, (slot + 1) * LANES)
                if entry < 0:
                    value = block_ref[h * groups, :, lanes].astype(F32)
                    biases_ref[:, columns] = value[0:3]
                    gains_ref[:, columns] = value[3:6]
                else:
                    value = block_ref[h * groups : (h + 1) * groups, :, lanes]
                    out_ref[entry, :, columns] = value.reshape(groups * TILE, LANES).astype(F32)
        if entry >= 0:
            out_ref.send(pl.ds(entry, 1))


def edge_backward_kernel(
    factor, n_band, count_ref, core_ref, band_ref, source_ref, target_ref, scaled_ref, w2, inverse_ref, normed_ref,
    hidden_ref, slope_ref, mesh_ref, tables, pre_grad_ref, grid_bias_ref, gains_ref, dec_gain_ref, *refs
):
    table_refs, refs = refs[:n_band], refs[n_band:]
    dst_ref, keep_ref, send_ref, dst_sum, weight_sum, small_sum, right_ref = refs
    mesh_rows = scaled_ref.shape[0]
    size = n_band * LANES
    dst_sum[...] = jnp.zeros(dst_sum.shape, F32)
    weight_sum[...] = jnp.zeros(weight_sum.shape, F32)
    scaled_ref, w2, source_ref, target_ref, inverse_ref = (
        item.get() for item in (scaled_ref, w2, source_ref, target_ref, inverse_ref)
    )

    def group(c, carry):
        for item in (normed_ref, hidden_ref, slope_ref):
            item.arrive(c)
        targets = live_rows(target_ref[c], count_ref[c])
        sources = (source_ref[c] - band_ref[0] * LANES) & (size - 1)
        rows = pl.ds(pl.multiple_of(c * 8 * LANES, 8 * LANES), 8 * LANES)
        scaled = dot(pick_matrix(as_columns(targets), 0, 8, mesh_rows), scaled_ref[...])
        inverse = rows_as_column(inverse_ref[c])
        grad_mixed = norm_backward(normed_ref[rows, :].astype(F32), inverse, scaled).astype(BF)
        weight_sum[...] += t_dot(hidden_ref[rows, :], grad_mixed)
        grad_pre = (dot_t(grad_mixed, w2[...]) * slope_ref[rows, :].astype(F32)).astype(BF)
        dst_sum[...] += dot(place_matrix(targets, 0, 8, mesh_rows), grad_pre)
        placed = dot(place_matrix(sources, 0, 8, size), grad_pre).astype(BF)
        right_ref[pl.ds(pl.multiple_of(c * size, size), size), :] = placed
        for j, table_ref in enumerate(table_refs):
            table_ref[c] = placed[j * LANES : (j + 1) * LANES, :]
        return carry

    lax.fori_loop(0, 3, group, 0)
    for table_ref in table_refs:
        table_ref.send()
    dst_grad = dst_sum[...].astype(BF)
    dst_ref[...] = dst_grad
    dst_ref.send()
    put_whole(factor, core_ref, weight_sum, keep_ref, send_ref, 2)
    put_outer(factor, core_ref, tables, right_ref, keep_ref, send_ref, 0, small_sum)
    put_outer(factor, core_ref, mesh_ref, dst_ref, keep_ref, send_ref, 1, weight_sum)
    small_sum[...] = jnp.zeros(small_sum.shape, F32)
    small_sum[0:1, :] = jnp.sum(dst_grad.astype(F32), axis=0, keepdims=True)
    small_sum[1:2, :] = jnp.sum(pre_grad_ref[...].astype(F32), axis=0, keepdims=True)
    small_sum[2:3, :] = grid_bias_ref[...]
    small_sum[3:5, :] = gains_ref[...]
    small_sum[5:6, :] = dec_gain_ref[...]
    put_whole(factor, core_ref, small_sum, keep_ref, send_ref, 3)


def band_sum_kernel(*refs):
    blocks, outs = refs[:-3], refs[-3:]
    for c in (0, 2, 1):
        total = blocks[0][c].astype(F32)
        for block_ref in blocks[1:]:
            total += block_ref[c].astype(F32)
        outs[c][...] = total.astype(BF)
        outs[c].send()


def final_kernel(
    pre_grad_ref, w3, dst_grad_ref, w1, new_grad_ref, index_ref, next_ref, own_ref, prev_ref, w0, grad_ref
):
    mesh_rows = new_grad_ref.shape[0]
    partial = new_grad_ref[...] + dot_t(pre_grad_ref[...], w3[...]) + dot_t(dst_grad_ref[...], w1[...])
    halo = jnp.concatenate([next_ref[...], own_ref[...], prev_ref[...]], axis=0)
    src_grad = dot(place_matrix(index_ref[...], 0, 3, mesh_rows), halo)
    grad_ref[...] = (partial + dot_t(src_grad.astype(BF), w0[...])).astype(BF)


def swap(value):
    return lax.ppermute(value, "core", [(0, 1), (1, 0)])


def pair(keep, got):
    return (keep.astype(F32) + got.astype(F32)).astype(BF)


def pad_rows(index, rows):
    return jnp.pad(index, ((0, rows - index.shape[0]), (0, 0)))


def body(
    mesh_latent, grid_latent, weights, biases, gains, cotangent, halo_index, edge_source, edge_target,
    block_count, decoder_send, decoder_source,
):
    n_band = lax.axis_size("z")
    n_mesh = lax.axis_size(("x", "y", "core"))
    n_x, plane = lax.axis_size("x"), lax.axis_size(("y", "z"))
    chips = n_x * plane
    own = PIECES // chips
    mesh_rows, features = mesh_latent.shape
    grid_rows = grid_latent.shape[0]
    shards, slots_each = decoder_send.shape[1:]
    slots = shards * slots_each
    edges = 3 * edge_source.shape[2] * edge_source.shape[3]
    square = 2 * features * features
    factor = 1.0 / math.sqrt(grid_rows * n_mesh * n_band)
    w = [(weights, k) for k in range(9)]
    core, band = lax.axis_index("core"), lax.axis_index("z")
    core_row, band_row = core[None], band[None]
    sources, targets, counts = edge_source[0], edge_target[0], block_count[0]
    wide, wide32 = ((mesh_rows, features), BF), ((mesh_rows, features), F32)
    block = ((LANES, features), BF)

    def half(count):
        return [((PIECES, TILE, count * LANES), BF)] * 2

    halo_rows = halo_index[0]
    outgoing = call(halo_kernel, [block] * 3, [mesh_latent, halo_rows], 384 * square)
    row = ("x", "y", "core")
    forward = [(i, (i + 1) % n_mesh) for i in range(n_mesh)]
    backward = [(i, (i - 1) % n_mesh) for i in range(n_mesh)]
    around = [[(i, (i - step) % n_band) for i in range(n_band)] for step in range(n_band)]
    own_rows = [outgoing[1]] + [lax.ppermute(outgoing[1], "z", route) for route in around[1:]]
    outer = jnp.concatenate([lax.ppermute(outgoing[0], row, backward), lax.ppermute(outgoing[2], row, forward)], axis=0)
    outer_rows = [outer] + [lax.ppermute(outer, "z", route) for route in around[1:]]
    tables = [(rows, 0) for rows in outer_rows] + [(rows, 0) for rows in own_rows] + [(rows, LANES) for rows in outer_rows]

    send_rows = decoder_send[0].reshape(slots // LANES, LANES)
    source_rows = pad_rows(decoder_source.reshape(3 * grid_rows // LANES, LANES), 16)
    small_inverse = ((mesh_rows // LANES, LANES), F32)
    (
        hidden, slope, normed, inverse, aggregate, node_hidden, node_slope, node_normed, node_inverse, new_mesh, outbound,
    ) = call(
        functools.partial(edge_forward_kernel, n_band),
        [
            ((edges, features), BF), ((edges, features), BF), ((edges, features), BF), (targets.shape, F32),
            wide, wide, wide, wide, small_inverse, wide, ((slots, features), BF),
        ],
        [counts, band_row, mesh_latent, w[1], tables]
        + [w[0], sources, targets, biases, w[2], w[3], w[4], w[5], w[6], gains, send_rows],
        5 * edges * square,
        [
            pltpu.VMEM((3 * n_band * LANES, features), BF), pltpu.VMEM((mesh_rows, features), BF),
            pltpu.VMEM((mesh_rows, features), F32),
        ],
    )
    received = lax.all_to_all(
        outbound.reshape(shards, slots_each, features), AXES, split_axis=0, concat_axis=0, tiled=True
    ).reshape(slots, features)
    slot_grad, proj_grad, dec_weight, dec_gain = call(
        decoder_kernel,
        [((slots, features), BF), ((grid_rows, features), BF), ((features, features), F32), ((1, features), F32)],
        [grid_latent, w[7], biases, cotangent, gains, source_rows, received, w[8]],
        7 * 3 * grid_rows * square,
        near=[received],
        loose=(0,),
    )
    returned = lax.all_to_all(
        slot_grad.reshape(shards, slots_each, features), AXES, split_axis=0, concat_axis=0, tiled=True
    ).reshape(slots, features)
    late_keep, late_send, grad_grid, grid_bias = call(
        functools.partial(grid_kernel, factor),
        half(2) + [((grid_rows, features), BF), ((1, features), F32)],
        [core_row, proj_grad, grid_latent, dec_weight, cotangent, w[7]],
        2 * grid_rows * square,
        [pltpu.VMEM((features, features), F32)],
    )
    late_got = swap(late_send)
    returned, late_sum = lax.optimization_barrier((returned, pair(late_keep, late_got)))
    new_grad, pre_grad, scaled, node_gains, node_keep, node_send = call(
        functools.partial(node_backward_kernel, factor),
        [wide32, wide, wide, ((2, features), F32)] + half(4),
        [
            core_row, send_rows, returned, w[6], node_normed, node_inverse, gains, w[5], node_slope, w[4],
            aggregate, mesh_latent, node_hidden, new_mesh,
        ],
        9 * mesh_rows * square,
        [
            pltpu.VMEM((mesh_rows, features), BF), pltpu.VMEM((mesh_rows, features), BF),
            pltpu.VMEM((features, features), F32),
        ],
        near=[returned],
    )
    early = jnp.concatenate([late_sum, pair(node_keep, swap(node_send))], axis=2)
    early = lax.all_to_all(early, CHIPS, split_axis=0, concat_axis=0, tiled=True)
    square_shape = (features, features)
    *table_grads, dst_grad, edge_keep, edge_send = call(
        functools.partial(edge_backward_kernel, factor, n_band),
        [((3, LANES, features), BF)] * n_band + [wide] + half(4),
        [
            counts, core_row, band_row, sources, targets, scaled, w[2], inverse, normed, hidden, slope, mesh_latent,
            tables, pre_grad, grid_bias, node_gains, dec_gain,
        ],
        7 * edges * square,
        [
            pltpu.VMEM((mesh_rows, features), F32), pltpu.VMEM(square_shape, F32), pltpu.VMEM(square_shape, F32),
            pltpu.VMEM((3 * n_band * LANES, features), BF),
        ],
        streams=(8, 9, 10),
        runs=3,
    )
    edge_got = swap(edge_send)
    edge_got, _ = lax.optimization_barrier((edge_got, early))
    late = pair(edge_keep, edge_got)
    late = lax.all_to_all(late, CHIPS, split_axis=0, concat_axis=0, tiled=True)
    (shared,) = call(
        functools.partial(share_kernel, chips), [((plane, own, TILE, 10 * LANES), BF)], [early, late], 0, near=[early, late], loose=(0,)
    )
    block_rows = lax.all_to_all(shared, ("y", "z"), split_axis=0, concat_axis=0, tiled=True)
    block_rows = block_rows.reshape(plane * own, TILE, 10 * LANES)
    late_grads, _ = lax.optimization_barrier((table_grads[1:], shared))
    swept = [table_grads[0]]
    for step in range(1, n_band):
        route = [(i, (i + step) % n_band) for i in range(n_band)]
        swept.append(lax.ppermute(late_grads[step - 1], "z", route))
    mine = jnp.broadcast_to(block_rows[None], (n_x,) + block_rows.shape)
    mine = lax.all_to_all(mine, "x", split_axis=0, concat_axis=0, tiled=True)
    mine = mine.reshape(PIECES, TILE, 10 * LANES)
    summed_next, summed_own, summed_prev = call(band_sum_kernel, [block] * 3, swept, 0)
    summed_next = lax.ppermute(summed_next, row, forward)
    summed_prev = lax.ppermute(summed_prev, row, backward)
    mine, _, _ = lax.optimization_barrier((mine, summed_next, summed_prev))
    other = swap(mine)
    (grad_mesh,) = call(
        final_kernel,
        [wide],
        [pre_grad, w[3], dst_grad, w[1], new_grad, halo_rows, summed_next, summed_own, summed_prev, w[0]],
        4 * mesh_rows * square,
    )
    grad_biases, grad_gains, grad_weights = call(
        functools.partial(spread_kernel, (6, 7, 8, 2, 3, 4, 5, 0, 1)),
        [((3, features), F32), ((3, features), F32), ((9, features, features), F32)],
        [core_row, mine, other],
        0,
        after=[grad_mesh],
        near=[mine, other],
    )
    return grad_mesh, grad_grid, grad_weights, grad_biases, grad_gains


def solution(mesh):
    n_mesh, n_band = mesh.devices.shape
    side = math.isqrt(n_mesh // 2)
    axes = jax.sharding.Mesh(mesh.devices.reshape(n_mesh // (2 * side), side, 2, n_band), AXES)
    both = P(AXES)
    return jax.shard_map(
        body,
        mesh=axes,
        in_specs=(both, both, P(), P(), P(), both, both, both, both, both, both, P(None, AXES)),
        out_specs=(both, both, P(), P(), P()),
        check_vma=False,
    )
```

```python
import functools
import math

import jax
import jax.numpy as jnp
from jax import lax
from jax.experimental import pallas as pl
from jax.experimental.pallas import tpu as pltpu
from jax.sharding import PartitionSpec as P

EPSILON = 1e-05
BF = jnp.bfloat16
F32 = jnp.float32
LANES = 128
TILE = 16
PIECES = 64
AXES = ("x", "y", "core", "z")
CHIPS = ("x", "y", "z")


def dot(left, right):
    return jnp.dot(left, right, preferred_element_type=F32)


def dot_t(left, right):
    return lax.dot_general(left, right, (((1,), (1,)), ((), ())), preferred_element_type=F32)


def t_dot(left, right):
    return lax.dot_general(left, right, (((0,), (0,)), ((), ())), preferred_element_type=F32)


def sigmoid(value):
    return 0.5 * jnp.tanh(0.5 * value) + 0.5


def row_mean(value):
    return jnp.mean(value, axis=-1, keepdims=True)


def norm_forward(mixed):
    centered = mixed - row_mean(mixed)
    inverse = lax.rsqrt(row_mean(centered * centered) + EPSILON)
    return centered * inverse, inverse


def norm_backward(normed, inverse, scaled):
    return inverse * (scaled - row_mean(scaled) - normed * row_mean(scaled * normed))


def one_hot(mask):
    return jnp.where(mask, 1.0, 0.0).astype(BF)


def as_columns(index):
    return jnp.transpose(index.astype(F32)).astype(jnp.int32)


def pick_matrix(columns, first, blocks, size):
    lanes = lax.broadcasted_iota(jnp.int32, (LANES, size), 1)
    parts = [one_hot(columns[:, b : b + 1] == lanes) for b in range(first, first + blocks)]
    return jnp.concatenate(parts, axis=0)


def place_matrix(rows, first, blocks, size):
    sublanes = lax.broadcasted_iota(jnp.int32, (size, LANES), 0)
    parts = [one_hot(rows[b : b + 1, :] == sublanes) for b in range(first, first + blocks)]
    return jnp.concatenate(parts, axis=1)


class Operand:
    def __init__(self, source, buffer, semaphore):
        self.source, self.buffer, self.semaphore = source, buffer, semaphore
        self.shape, self.dtype = buffer.shape, buffer.dtype
        self.arrived = False

    def copies(self):
        if not isinstance(self.source, list):
            return [pltpu.make_async_copy(self.source, self.buffer, self.semaphore.at[0])]
        size = self.shape[0] // len(self.source)
        return [
            pltpu.make_async_copy(source, self.buffer.at[pl.ds(k * size, size)], self.semaphore.at[k])
            for k, source in enumerate(self.source)
        ]

    def start(self):
        for copy in self.copies():
            copy.start()

    def get(self):
        if not self.arrived:
            for copy in self.copies():
                copy.wait()
            self.arrived = True
        return self.buffer

    def __getitem__(self, index):
        return self.get()[index]


class Stream(Operand):
    def run(self, number):
        count = self.semaphore.shape[0]
        size = self.shape[0] // count
        rows = pl.ds(number * size if isinstance(number, int) else pl.multiple_of(number * size, size), size)
        return pltpu.make_async_copy(self.source.at[rows], self.buffer.at[rows], self.semaphore.at[number])

    def arrive(self, number):
        self.run(number).wait()

    def get(self):
        return self.buffer


class Result:
    def __init__(self, target, buffer, semaphore):
        self.target, self.buffer, self.semaphore = target, buffer, semaphore
        self.shape, self.dtype = buffer.shape, buffer.dtype
        self.sent = False

    def __getitem__(self, index):
        return self.buffer[index]

    def __setitem__(self, index, value):
        self.buffer[index] = value

    def send(self, rows=None):
        self.sent = True
        if rows is None:
            pltpu.make_async_copy(self.buffer, self.target, self.semaphore).start()
        else:
            pltpu.make_async_copy(self.buffer.at[rows], self.target.at[rows], self.semaphore).start()

    def finish(self):
        if not self.sent:
            self.send()
        pltpu.make_async_copy(self.buffer, self.target, self.semaphore).wait()


def call(kernel, outs, args, flops, scratch=(), streams=(), runs=1, after=(), near=(), loose=()):
    arrays, places, shapes, kinds = [], [], [], []

    def place(array):
        for k, other in enumerate(arrays):
            if other is array:
                return k
        arrays.append(array)
        return len(arrays) - 1

    for arg in args:
        if isinstance(arg, list):
            places.append([(place(array), start) for array, start in arg])
            shapes.append((len(arg) * LANES,) + arg[0][0].shape[1:])
            kinds.append(arg[0][0].dtype)
            continue
        array, entry = arg if isinstance(arg, tuple) else (arg, None)
        places.append((place(array), entry))
        shapes.append(array.shape if entry is None else array.shape[1:])
        kinds.append(array.dtype)
    scalar = [len(shape) == 1 for shape in shapes]
    buffers, semaphores = [], []
    for number, where in enumerate(places):
        if not scalar[number]:
            buffers.append(pltpu.VMEM(shapes[number], kinds[number]))
            count = len(where) if isinstance(where, list) else runs if number in streams else 1
            semaphores.append(pltpu.SemaphoreType.DMA((count,)))
    for array in after:
        place(array)
    out_shapes = [
        (pltpu.HBM if near and number not in loose else jax.ShapeDtypeStruct)(shape, kind)
        for number, (shape, kind) in enumerate(outs)
    ]
    out_buffers = [pltpu.VMEM(shape, kind) for shape, kind in outs]
    operands = arrays
    n_in, n_out, n_buf = len(operands), len(out_shapes), len(buffers)

    def wrapped(*refs):
        sources, targets = refs[:n_in], refs[n_in : n_in + n_out]
        rest = refs[n_in + n_out :]
        in_buffers, rest = rest[:n_buf], rest[n_buf:]
        out_refs, rest = rest[:n_out], rest[n_out:]
        in_semaphores, rest = rest[:n_buf], rest[n_buf:]
        out_semaphore, user = rest[0], rest[1:]
        inputs, position = [], 0
        for number, where in enumerate(places):
            if scalar[number]:
                inputs.append(sources[where[0]])
                continue
            if isinstance(where, list):
                source = [sources[k].at[pl.ds(start, LANES)] for k, start in where]
            else:
                source = sources[where[0]] if where[1] is None else sources[where[0]].at[where[1]]
            kind = Stream if number in streams else Operand
            inputs.append(kind(source, in_buffers[position], in_semaphores[position]))
            position += 1
        for item in inputs:
            if isinstance(item, Operand) and not isinstance(item, Stream):
                item.start()
        for number in range(runs if streams else 0):
            for item in inputs:
                if isinstance(item, Stream):
                    item.run(number).start()
        results = []
        for number in range(n_out):
            results.append(Result(targets[number], out_refs[number], out_semaphore.at[number]))
        kernel(*inputs, *results, *user)
        for item in inputs:
            if isinstance(item, Operand) and not isinstance(item, Stream):
                item.get()
        for item in results:
            item.finish()

    moved = sum(math.prod(s) * t.itemsize for s, t in zip(shapes, kinds))
    moved += sum(math.prod(s) * jnp.dtype(t).itemsize for s, t in outs)
    return pl.pallas_call(
        wrapped,
        out_shape=out_shapes,
        in_specs=[pl.BlockSpec(memory_space=pltpu.SMEM if a.ndim == 1 else pl.ANY) for a in operands],
        out_specs=[pl.BlockSpec(memory_space=pl.ANY)] * n_out,
        scratch_shapes=buffers + out_buffers + semaphores + [pltpu.SemaphoreType.DMA((n_out,))] + list(scratch),
        compiler_params=pltpu.CompilerParams(vmem_limit_bytes=(36 if near else 56) * 1024 * 1024),
        cost_estimate=pl.CostEstimate(flops=flops, bytes_accessed=moved, transcendentals=0),
    )(
        *[
            a if a.ndim == 1 or any(a is b for b in near) else pltpu.with_memory_space_constraint(a, pltpu.HBM)
            for a in operands
        ]
    )


def halo_kernel(mesh_ref, index_ref, *out_refs):
    index = index_ref[...]
    for c in (1, 0, 2):
        out_refs[c][...] = t_dot(place_matrix(index, c, 1, mesh_ref.shape[0]), mesh_ref[...]).astype(BF)
        out_refs[c].send()


def diagonal():
    shape = (LANES, LANES)
    return lax.broadcasted_iota(jnp.int32, shape, 0) == lax.broadcasted_iota(jnp.int32, shape, 1)


def column_as_rows(column):
    parts = [column[k : k + LANES] for k in range(0, column.shape[0], LANES)]
    return jnp.concatenate(
        [jnp.sum(jnp.where(diagonal(), part, 0.0), axis=0, keepdims=True) for part in parts], axis=0
    )


def rows_as_column(rows):
    parts = [rows[k : k + 1] for k in range(rows.shape[0])]
    return jnp.concatenate(
        [jnp.sum(jnp.where(diagonal(), part, 0.0), axis=1, keepdims=True) for part in parts], axis=0
    )


def live_rows(index, count):
    blocks = lax.broadcasted_iota(jnp.int32, index.shape, 0)
    return jnp.where(blocks < count, index, -1)


def edge_forward_kernel(
    n_band, count_ref, band_ref, mesh_ref, w1, tables, w0, source_ref, target_ref, biases, w2, w3, w4, w5, w6, gains,
    send_ref, hidden_ref, slope_ref, normed_ref, inverse_ref, aggregate_ref, node_hidden_ref, node_slope_ref,
    node_normed_ref, node_inverse_ref, new_mesh_ref, outbound_ref, table_ref, dst_ref, summed_ref,
):
    mesh_rows = mesh_ref.shape[0]
    size = n_band * LANES
    dst_ref[...] = (dot(mesh_ref[...], w1[...]) + biases[0:1, :]).astype(BF)
    table_ref[...] = dot(tables[...], w0[...]).astype(BF)
    summed_ref[...] = jnp.zeros(summed_ref.shape, F32)
    w2, source_ref, target_ref = w2.get(), source_ref.get(), target_ref.get()

    def group(c, carry):
        source_columns = as_columns((source_ref[c] - band_ref[0] * LANES) & (size - 1))
        targets = live_rows(target_ref[c], count_ref[c])
        target_columns = as_columns(targets)
        table = table_ref[pl.ds(pl.multiple_of(c * size, size), size), :]
        preact = dot(pick_matrix(source_columns, 0, 8, size), table)
        preact += dot(pick_matrix(target_columns, 0, 8, mesh_rows), dst_ref[...])
        gate = sigmoid(preact)
        hidden = (preact * gate).astype(BF)
        normed, inverse = norm_forward(dot(hidden, w2[...]))
        normed = normed.astype(BF)
        rows = pl.ds(pl.multiple_of(c * 8 * LANES, 8 * LANES), 8 * LANES)
        hidden_ref[rows, :] = hidden
        slope_ref[rows, :] = (gate * (1.0 + preact * (1.0 - gate))).astype(BF)
        normed_ref[rows, :] = normed
        inverse_ref[c] = column_as_rows(inverse)
        summed_ref[...] += dot(place_matrix(targets, 0, 8, mesh_rows), normed)
        for out_ref in (hidden_ref, slope_ref, normed_ref):
            out_ref.send(rows)
        return carry

    lax.fori_loop(0, 3, group, 0)
    for out_ref in (hidden_ref, slope_ref, normed_ref):
        out_ref.sent = True
    w3, w4, w5, w6, gains, send_ref = (item.get() for item in (w3, w4, w5, w6, gains, send_ref))
    aggregate = (summed_ref[...] * gains[0:1, :]).astype(BF)
    aggregate_ref[...] = aggregate
    node_pre = dot(mesh_ref[...], w3[...]) + biases[1:2, :] + dot(aggregate, w4[...])
    gate = sigmoid(node_pre)
    node_hidden = (node_pre * gate).astype(BF)
    node_hidden_ref[...] = node_hidden
    node_slope_ref[...] = (gate * (1.0 + node_pre * (1.0 - gate))).astype(BF)
    normed, inverse = norm_forward(dot(node_hidden, w5[...]))
    node_normed_ref[...] = normed.astype(BF)
    node_inverse_ref[...] = column_as_rows(inverse)
    new_mesh = (mesh_ref[...].astype(F32) + normed * gains[1:2, :]).astype(BF)
    new_mesh_ref[...] = new_mesh
    for out_ref in (aggregate_ref, node_hidden_ref, node_slope_ref, node_normed_ref, node_inverse_ref, new_mesh_ref):
        out_ref.send()
    value = dot(new_mesh, w6[...]).astype(BF)
    outbound_ref[...] = dot(pick_matrix(as_columns(send_ref[...]), 0, 8, mesh_rows), value).astype(BF)


def decoder_kernel(
    grid_ref, w7, biases, cot_ref, gains, source_ref, received_ref, w8,
    slot_ref, proj_grad_ref, weight_ref, gain_ref,
):
    slots = received_ref.shape[0]
    rows = grid_ref.shape[0]
    for item in (grid_ref, w7, biases, cot_ref, gains, source_ref, received_ref, w8):
        item.get()
    proj = (dot(grid_ref[...], w7[...]) + biases[2:3, :]).astype(BF).astype(F32)
    cot = cot_ref[...].astype(F32)
    cot = jnp.concatenate([cot] * 3, axis=0)
    preact = dot(pick_matrix(as_columns(source_ref[...]), 0, 12, slots), received_ref[...])
    preact += jnp.concatenate([proj] * 3, axis=0)
    gate = sigmoid(preact)
    hidden = (preact * gate).astype(BF)
    slope = gate * (1.0 + preact * (1.0 - gate))
    normed, inverse = norm_forward(dot(hidden, w8[...]))
    grad_mixed = norm_backward(normed, inverse, cot * gains[2:3, :]).astype(BF)
    gain_ref[...] = jnp.sum(cot * normed, axis=0, keepdims=True)
    grad_pre = (dot_t(grad_mixed, w8[...]) * slope).astype(BF)
    slot_ref[...] = dot(place_matrix(source_ref[...], 0, 12, slots), grad_pre).astype(BF)
    slot_ref.send()
    wide = grad_pre.astype(F32)
    proj_grad_ref[...] = (wide[:rows] + wide[rows : 2 * rows] + wide[2 * rows :]).astype(BF)
    proj_grad_ref.send()
    weight_ref[...] = t_dot(hidden, grad_mixed)


def put_pieces(out_ref, slot, value):
    rounded = value.astype(BF)
    groups = value.shape[0] // TILE
    for h in range(2):
        block = rounded[:, h * LANES : (h + 1) * LANES].reshape(groups, TILE, LANES)
        out_ref[h * groups : (h + 1) * groups, :, slot * LANES : (slot + 1) * LANES] = block


def split_columns(core_ref, size):
    half = size // 2
    mine = core_ref[0] * half
    return pl.ds(pl.multiple_of(mine, half), half), pl.ds(pl.multiple_of(half - mine, half), half)


def put_whole(factor, core_ref, value_ref, keep_ref, send_ref, slot):
    for columns, out_ref in zip(split_columns(core_ref, value_ref.shape[1]), (keep_ref, send_ref)):
        put_pieces(out_ref, slot, value_ref[:, columns] * factor)


def put_outer(factor, core_ref, left_ref, right_ref, keep_ref, send_ref, slot, product_ref):
    product_ref[...] = t_dot(left_ref[...], right_ref[...])
    put_whole(factor, core_ref, product_ref, keep_ref, send_ref, slot)


def grid_kernel(
    factor, core_ref, proj_grad_ref, grid_ref, dec_weight, cot_ref, w7, keep_ref, send_ref, grad_ref, bias_ref,
    product_ref,
):
    put_outer(factor, core_ref, grid_ref, proj_grad_ref, keep_ref, send_ref, 0, product_ref)
    put_whole(factor, core_ref, dec_weight, keep_ref, send_ref, 1)
    keep_ref.send()
    send_ref.send()
    proj_grad = proj_grad_ref[...]
    grad_ref[...] = (cot_ref[...].astype(F32) + dot_t(proj_grad, w7[...])).astype(BF)
    grad_ref.send()
    bias_ref[...] = jnp.sum(proj_grad.astype(F32), axis=0, keepdims=True)


def node_backward_kernel(
    factor, core_ref, send_ref, returned_ref, w6, node_normed_ref, node_inverse_ref, gains, w5, node_slope_ref, w4,
    aggregate_ref, mesh_ref, node_hidden_ref, new_mesh_ref, late_ref,
    new_grad_ref, pre_grad_ref, scaled_ref, gain_ref, out_keep, out_send, value_grad_ref, out_grad_ref,
    product_ref,
):
    mesh_rows = node_normed_ref.shape[0]
    value_grad = dot(place_matrix(send_ref[...], 0, 8, mesh_rows), returned_ref[...]).astype(BF)
    value_grad_ref[...] = value_grad
    new_grad = dot_t(value_grad, w6[...])
    new_grad_ref[...] = new_grad
    normed = node_normed_ref[...].astype(F32)
    inverse = rows_as_column(node_inverse_ref[...])
    out_grad = norm_backward(normed, inverse, new_grad * gains[1:2, :]).astype(BF)
    out_grad_ref[...] = out_grad
    pre_grad = (dot_t(out_grad, w5[...]) * node_slope_ref[...].astype(F32)).astype(BF)
    pre_grad_ref[...] = pre_grad
    aggregate_grad = dot_t(pre_grad, w4[...])
    scaled_ref[...] = (aggregate_grad * gains[0:1, :]).astype(BF)
    summed = aggregate_ref[...].astype(F32)
    gain_ref[0:1, :] = jnp.sum(aggregate_grad * summed, axis=0, keepdims=True) / gains[0:1, :]
    gain_ref[1:2, :] = jnp.sum(new_grad * normed, axis=0, keepdims=True)
    for item in (new_grad_ref, pre_grad_ref, scaled_ref):
        item.send()
    put_outer(factor, core_ref, mesh_ref, pre_grad_ref, out_keep, out_send, 0, product_ref)
    put_outer(factor, core_ref, aggregate_ref, pre_grad_ref, out_keep, out_send, 1, product_ref)
    put_outer(factor, core_ref, node_hidden_ref, out_grad_ref, out_keep, out_send, 2, product_ref)
    put_outer(factor, core_ref, new_mesh_ref, value_grad_ref, out_keep, out_send, 3, product_ref)
    out_keep[:, :, 4 * LANES :] = late_ref[...]


def share_kernel(chips, *refs):
    out_ref = refs[-1]
    own = PIECES // chips
    first = 0
    for got_ref in refs[:-1]:
        got_ref = got_ref.get()
        width = got_ref.shape[2]
        total = got_ref[0:own].astype(F32)
        for k in range(1, chips):
            total += got_ref[k * own : (k + 1) * own].astype(F32)
        rounded = total.astype(BF)
        for copy in range(out_ref.shape[0]):
            out_ref[copy, :, :, first : first + width] = rounded
        first += width


def spread_kernel(slots, core_ref, mine_ref, other_ref, biases_ref, gains_ref, out_ref):
    groups = out_ref.shape[1] // TILE
    count = len(slots)
    mine_ref, other_ref = mine_ref.get(), other_ref.get()
    for entry in range(-1, count):
        slot = slots[entry] if entry >= 0 else count
        for start, block_ref in ((core_ref[0] * 2, mine_ref), (2 - core_ref[0] * 2, other_ref)):
            for h in range(2):
                columns = pl.ds(pl.multiple_of((start + h) * LANES, LANES), LANES)
                lanes = slice(slot * LANES, (slot + 1) * LANES)
                if entry < 0:
                    value = block_ref[h * groups, :, lanes].astype(F32)
                    biases_ref[:, columns] = value[0:3]
                    gains_ref[:, columns] = value[3:6]
                else:
                    value = block_ref[h * groups : (h + 1) * groups, :, lanes]
                    out_ref[entry, :, columns] = value.reshape(groups * TILE, LANES).astype(F32)
        if entry >= 0:
            out_ref.send(pl.ds(entry, 1))


def edge_backward_kernel(
    factor, n_band, count_ref, core_ref, band_ref, source_ref, target_ref, scaled_ref, w2, inverse_ref, normed_ref,
    hidden_ref, slope_ref, mesh_ref, tables, pre_grad_ref, grid_bias_ref, gains_ref, dec_gain_ref, *refs
):
    table_refs, refs = refs[:n_band], refs[n_band:]
    dst_ref, keep_ref, send_ref, dst_sum, weight_sum, small_sum, right_ref = refs
    mesh_rows = scaled_ref.shape[0]
    size = n_band * LANES
    dst_sum[...] = jnp.zeros(dst_sum.shape, F32)
    weight_sum[...] = jnp.zeros(weight_sum.shape, F32)
    scaled_ref, w2, source_ref, target_ref, inverse_ref = (
        item.get() for item in (scaled_ref, w2, source_ref, target_ref, inverse_ref)
    )

    def group(c, carry):
        for item in (normed_ref, hidden_ref, slope_ref):
            item.arrive(c)
        targets = live_rows(target_ref[c], count_ref[c])
        sources = (source_ref[c] - band_ref[0] * LANES) & (size - 1)
        rows = pl.ds(pl.multiple_of(c * 8 * LANES, 8 * LANES), 8 * LANES)
        scaled = dot(pick_matrix(as_columns(targets), 0, 8, mesh_rows), scaled_ref[...])
        inverse = rows_as_column(inverse_ref[c])
        grad_mixed = norm_backward(normed_ref[rows, :].astype(F32), inverse, scaled).astype(BF)
        weight_sum[...] += t_dot(hidden_ref[rows, :], grad_mixed)
        grad_pre = (dot_t(grad_mixed, w2[...]) * slope_ref[rows, :].astype(F32)).astype(BF)
        dst_sum[...] += dot(place_matrix(targets, 0, 8, mesh_rows), grad_pre)
        placed = dot(place_matrix(sources, 0, 8, size), grad_pre).astype(BF)
        right_ref[pl.ds(pl.multiple_of(c * size, size), size), :] = placed
        for j, table_ref in enumerate(table_refs):
            table_ref[c] = placed[j * LANES : (j + 1) * LANES, :]
        return carry

    lax.fori_loop(0, 3, group, 0)
    for table_ref in table_refs:
        table_ref.send()
    dst_grad = dst_sum[...].astype(BF)
    dst_ref[...] = dst_grad
    dst_ref.send()
    put_whole(factor, core_ref, weight_sum, keep_ref, send_ref, 2)
    put_outer(factor, core_ref, tables, right_ref, keep_ref, send_ref, 0, small_sum)
    put_outer(factor, core_ref, mesh_ref, dst_ref, keep_ref, send_ref, 1, weight_sum)
    small_sum[...] = jnp.zeros(small_sum.shape, F32)
    small_sum[0:1, :] = jnp.sum(dst_grad.astype(F32), axis=0, keepdims=True)
    small_sum[1:2, :] = jnp.sum(pre_grad_ref[...].astype(F32), axis=0, keepdims=True)
    small_sum[2:3, :] = grid_bias_ref[...]
    small_sum[3:5, :] = gains_ref[...]
    small_sum[5:6, :] = dec_gain_ref[...]
    put_whole(factor, core_ref, small_sum, keep_ref, send_ref, 3)


def band_sum_kernel(*refs):
    blocks, outs = refs[:-3], refs[-3:]
    for c in (0, 2, 1):
        total = blocks[0][c].astype(F32)
        for block_ref in blocks[1:]:
            total += block_ref[c].astype(F32)
        outs[c][...] = total.astype(BF)
        outs[c].send()


def final_kernel(
    pre_grad_ref, w3, dst_grad_ref, w1, new_grad_ref, index_ref, next_ref, own_ref, prev_ref, w0, grad_ref
):
    mesh_rows = new_grad_ref.shape[0]
    partial = new_grad_ref[...] + dot_t(pre_grad_ref[...], w3[...]) + dot_t(dst_grad_ref[...], w1[...])
    halo = jnp.concatenate([next_ref[...], own_ref[...], prev_ref[...]], axis=0)
    src_grad = dot(place_matrix(index_ref[...], 0, 3, mesh_rows), halo)
    grad_ref[...] = (partial + dot_t(src_grad.astype(BF), w0[...])).astype(BF)


def swap(value):
    return lax.ppermute(value, "core", [(0, 1), (1, 0)])


def pair(keep, got):
    return (keep.astype(F32) + got.astype(F32)).astype(BF)


def pad_rows(index, rows):
    return jnp.pad(index, ((0, rows - index.shape[0]), (0, 0)))


def body(
    mesh_latent, grid_latent, weights, biases, gains, cotangent, halo_index, edge_source, edge_target,
    block_count, decoder_send, decoder_source,
):
    n_band = lax.axis_size("z")
    n_mesh = lax.axis_size(("x", "y", "core"))
    n_x, plane = lax.axis_size("x"), lax.axis_size(("y", "z"))
    chips = n_x * plane
    own = PIECES // chips
    mesh_rows, features = mesh_latent.shape
    grid_rows = grid_latent.shape[0]
    shards, slots_each = decoder_send.shape[1:]
    slots = shards * slots_each
    edges = 3 * edge_source.shape[2] * edge_source.shape[3]
    square = 2 * features * features
    factor = 1.0 / math.sqrt(grid_rows * n_mesh * n_band)
    w = [(weights, k) for k in range(9)]
    core, band = lax.axis_index("core"), lax.axis_index("z")
    core_row, band_row = core[None], band[None]
    sources, targets, counts = edge_source[0], edge_target[0], block_count[0]
    wide, wide32 = ((mesh_rows, features), BF), ((mesh_rows, features), F32)
    block = ((LANES, features), BF)

    def half(count):
        return [((PIECES, TILE, count * LANES), BF)] * 2

    halo_rows = halo_index[0]
    outgoing = call(halo_kernel, [block] * 3, [mesh_latent, halo_rows], 384 * square)
    row = ("x", "y", "core")
    forward = [(i, (i + 1) % n_mesh) for i in range(n_mesh)]
    backward = [(i, (i - 1) % n_mesh) for i in range(n_mesh)]
    around = [[(i, (i - step) % n_band) for i in range(n_band)] for step in range(n_band)]
    own_rows = [outgoing[1]] + [lax.ppermute(outgoing[1], "z", route) for route in around[1:]]
    outer = jnp.concatenate([lax.ppermute(outgoing[0], row, backward), lax.ppermute(outgoing[2], row, forward)], axis=0)
    outer_rows = [outer] + [lax.ppermute(outer, "z", route) for route in around[1:]]
    tables = [(rows, 0) for rows in outer_rows] + [(rows, 0) for rows in own_rows] + [(rows, LANES) for rows in outer_rows]

    send_rows = decoder_send[0].reshape(slots // LANES, LANES)
    source_rows = pad_rows(decoder_source.reshape(3 * grid_rows // LANES, LANES), 16)
    small_inverse = ((mesh_rows // LANES, LANES), F32)
    (
        hidden, slope, normed, inverse, aggregate, node_hidden, node_slope, node_normed, node_inverse, new_mesh, outbound,
    ) = call(
        functools.partial(edge_forward_kernel, n_band),
        [
            ((edges, features), BF), ((edges, features), BF), ((edges, features), BF), (targets.shape, F32),
            wide, wide, wide, wide, small_inverse, wide, ((slots, features), BF),
        ],
        [counts, band_row, mesh_latent, w[1], tables]
        + [w[0], sources, targets, biases, w[2], w[3], w[4], w[5], w[6], gains, send_rows],
        5 * edges * square,
        [
            pltpu.VMEM((3 * n_band * LANES, features), BF), pltpu.VMEM((mesh_rows, features), BF),
            pltpu.VMEM((mesh_rows, features), F32),
        ],
    )
    received = lax.all_to_all(
        outbound.reshape(shards, slots_each, features), AXES, split_axis=0, concat_axis=0, tiled=True
    ).reshape(slots, features)
    slot_grad, proj_grad, dec_weight, dec_gain = call(
        decoder_kernel,
        [((slots, features), BF), ((grid_rows, features), BF), ((features, features), F32), ((1, features), F32)],
        [grid_latent, w[7], biases, cotangent, gains, source_rows, received, w[8]],
        7 * 3 * grid_rows * square,
        near=[received],
        loose=(0,),
    )
    returned = lax.all_to_all(
        slot_grad.reshape(shards, slots_each, features), AXES, split_axis=0, concat_axis=0, tiled=True
    ).reshape(slots, features)
    late_keep, late_send, grad_grid, grid_bias = call(
        functools.partial(grid_kernel, factor),
        half(2) + [((grid_rows, features), BF), ((1, features), F32)],
        [core_row, proj_grad, grid_latent, dec_weight, cotangent, w[7]],
        2 * grid_rows * square,
        [pltpu.VMEM((features, features), F32)],
    )
    late_got = swap(late_send)
    returned, late_sum = lax.optimization_barrier((returned, pair(late_keep, late_got)))
    new_grad, pre_grad, scaled, node_gains, node_keep, node_send = call(
        functools.partial(node_backward_kernel, factor),
        [wide32, wide, wide, ((2, features), F32)] + half(6)[:1] + half(4)[:1],
        [
            core_row, send_rows, returned, w[6], node_normed, node_inverse, gains, w[5], node_slope, w[4],
            aggregate, mesh_latent, node_hidden, new_mesh, late_sum,
        ],
        9 * mesh_rows * square,
        [
            pltpu.VMEM((mesh_rows, features), BF), pltpu.VMEM((mesh_rows, features), BF),
            pltpu.VMEM((features, features), F32),
        ],
        near=[returned],
    )
    early = pair(node_keep, jnp.pad(swap(node_send), ((0, 0), (0, 0), (0, 2 * LANES))))
    early = lax.all_to_all(early, CHIPS, split_axis=0, concat_axis=0, tiled=True)
    square_shape = (features, features)
    *table_grads, dst_grad, edge_keep, edge_send = call(
        functools.partial(edge_backward_kernel, factor, n_band),
        [((3, LANES, features), BF)] * n_band + [wide] + half(4),
        [
            counts, core_row, band_row, sources, targets, scaled, w[2], inverse, normed, hidden, slope, mesh_latent,
            tables, pre_grad, grid_bias, node_gains, dec_gain,
        ],
        7 * edges * square,
        [
            pltpu.VMEM((mesh_rows, features), F32), pltpu.VMEM(square_shape, F32), pltpu.VMEM(square_shape, F32),
            pltpu.VMEM((3 * n_band * LANES, features), BF),
        ],
        streams=(8, 9, 10),
        runs=3,
    )
    edge_got = swap(edge_send)
    edge_got, _ = lax.optimization_barrier((edge_got, early))
    late = pair(edge_keep, edge_got)
    late = lax.all_to_all(late, CHIPS, split_axis=0, concat_axis=0, tiled=True)
    (shared,) = call(
        functools.partial(share_kernel, chips), [((plane, own, TILE, 10 * LANES), BF)], [early, late], 0, near=[early, late], loose=(0,)
    )
    block_rows = lax.all_to_all(shared, ("y", "z"), split_axis=0, concat_axis=0, tiled=True)
    block_rows = block_rows.reshape(plane * own, TILE, 10 * LANES)
    late_grads, _ = lax.optimization_barrier((table_grads[1:], shared))
    swept = [table_grads[0]]
    for step in range(1, n_band):
        route = [(i, (i + step) % n_band) for i in range(n_band)]
        swept.append(lax.ppermute(late_grads[step - 1], "z", route))
    mine = jnp.broadcast_to(block_rows[None], (n_x,) + block_rows.shape)
    mine = lax.all_to_all(mine, "x", split_axis=0, concat_axis=0, tiled=True)
    mine = mine.reshape(PIECES, TILE, 10 * LANES)
    summed_next, summed_own, summed_prev = call(band_sum_kernel, [block] * 3, swept, 0)
    summed_next = lax.ppermute(summed_next, row, forward)
    summed_prev = lax.ppermute(summed_prev, row, backward)
    mine, _, _ = lax.optimization_barrier((mine, summed_next, summed_prev))
    other = swap(mine)
    (grad_mesh,) = call(
        final_kernel,
        [wide],
        [pre_grad, w[3], dst_grad, w[1], new_grad, halo_rows, summed_next, summed_own, summed_prev, w[0]],
        4 * mesh_rows * square,
    )
    grad_biases, grad_gains, grad_weights = call(
        functools.partial(spread_kernel, (6, 7, 8, 0, 1, 2, 3, 4, 5)),
        [((3, features), F32), ((3, features), F32), ((9, features, features), F32)],
        [core_row, mine, other],
        0,
        after=[grad_mesh],
        near=[mine, other],
    )
    return grad_mesh, grad_grid, grad_weights, grad_biases, grad_gains


def solution(mesh):
    n_mesh, n_band = mesh.devices.shape
    side = math.isqrt(n_mesh // 2)
    axes = jax.sharding.Mesh(mesh.devices.reshape(n_mesh // (2 * side), side, 2, n_band), AXES)
    both = P(AXES)
    return jax.shard_map(
        body,
        mesh=axes,
        in_specs=(both, both, P(), P(), P(), both, both, both, both, both, both, P(None, AXES)),
        out_specs=(both, both, P(), P(), P()),
        check_vma=False,
    )
```
